32 devices in a mesh: pts: 8 (over y, x, core), orb: 4 (over z).
Axes of the slice: x: 2, y: 2, z: 4, core: 2. Of those that a mesh axis runs over, the one named last changes fastest.
Arguments:
- amplitudes: float32 [64, 512, 512], P(None, 'orb'), may hold values from -6 to 6
- valence_points: float32 [512, 16384], P('orb', 'pts'), may hold values from -0.4 to 0.4
- conduction_points: float32 [512, 16384], P(None, 'pts'), may hold values from -0.4 to 0.4
- screened: float32 [16384, 16384], P('pts', 'orb'), may hold values from -0.0625 to 0.0625
- valence_energy: float32 [512], P('orb'), may hold values from -1.5 to -0.5
- conduction_energy: float32 [512], replicated, may hold values from 0.5 to 2.5
Outputs:
- second_step: float32 [64, 512, 512], P(None, 'orb')
The draws below stay inside these ranges and needn't reach their ends.
All inputs are finite; a program needn't handle non-finite values.
Results may differ from the reference program's by a relative error of at most 0.000078.
Values sent between devices are 32-bit elements; how exact they have to be, the bound alone decides.
No kernel may reach another device: no remote copies, remote signals or barrier semaphores. Data moves between devices by JAX's collectives and lax.ppermute only.
A program may use at most 256 MiB of HBM per device.

```python
import jax
import jax.numpy as jnp
from jax import lax

V = 512
C = 512
P_SIZE = 16384
B = 64


def spiked(values, rng, source, target, blocks, factor):
    def block_of(dim):
        return (jnp.arange(values.shape[dim]) // (values.shape[dim] // blocks)).reshape((-1,) + (1,) * (values.ndim - 1 - dim))

    first = jax.random.permutation(rng, blocks)[block_of(target)]
    second = (block_of(target) + blocks // 2) % blocks
    return jnp.where((block_of(source) == first) | (block_of(source) == second), factor * values, values)


def steps_of(key, extent, cuts, low, high):
    level = 1.0
    for position, blocks in cuts:
        heights = jax.random.uniform(jax.random.fold_in(jax.random.fold_in(key, 6), position), (blocks,), jnp.float32, low / len(cuts), high / len(cuts))
        level = level * jnp.repeat(jnp.exp(heights), extent[position] // blocks).reshape((-1,) + (1,) * (len(extent) - 1 - position))
    return level


def normal_values(stream_key, extent, deviation, most, split=(), dtype=jnp.bfloat16):
    drawn = deviation * jax.random.normal(stream_key, extent, jnp.float32)
    if split:
        drawn = drawn * steps_of(stream_key, extent, split, -0.22, 0.18)
    return jnp.clip(drawn, -most, most).astype(dtype)


def heavy_noise(own_key, dims, scale, reach, cuts, heavy, kind=jnp.bfloat16):
    result = scale * jax.random.normal(own_key, dims, jnp.float32)
    if cuts:
        result = result * steps_of(own_key, dims, cuts, -0.22, 0.18)
    return jnp.clip(spiked(result, jax.random.fold_in(own_key, 3), *heavy), -reach, reach).astype(kind)


def setup_inputs(seed: int = 0) -> dict:
    splits = jax.random.split(jax.random.key(seed), 7)
    return {
        "amplitudes": normal_values(splits[0], (B, V, C), 1.0, 6.0, ((1, 4),), jnp.float32),
        "valence_points": normal_values(splits[1], (V, P_SIZE), 0.0625, 0.4, ((0, 4), (1, 8)), jnp.float32),
        "conduction_points": normal_values(splits[2], (C, P_SIZE), 0.0625, 0.4, ((1, 8),), jnp.float32),
        "screened": heavy_noise(splits[3], (P_SIZE, P_SIZE), P_SIZE ** -0.5, 0.0625, ((0, 8), (1, 4)), (1, 0, 8, 2.0), jnp.float32),
        "valence_energy": jnp.clip(-1.5 + 1.0 * jax.random.uniform(splits[4], (V,), jnp.float32) ** steps_of(splits[4], (V,), ((0, 4),), -0.2, 0.2), -1.5, -0.5),
        "conduction_energy": jnp.clip(jax.random.uniform(splits[5], (C,), jnp.float32, 0.5, 2.5), 0.5, 2.5),
    }


center_shift = 2.5
highest = lax.Precision.HIGHEST


def apply_kernel(block, valence_points, conduction_points, screened):
    def encode_one(vectors):
        prod = jnp.dot(vectors, conduction_points, precision=highest, preferred_element_type=jnp.float32)
        return jnp.sum(prod * valence_points, axis=0)

    encoded = lax.map(encode_one, block)
    interacted = lax.dot_general(encoded, screened, (((1,), (1,)), ((), ())), precision=highest, preferred_element_type=jnp.float32)

    def decode_one(row):
        weighted = valence_points * row[None, :]
        return lax.dot_general(weighted, conduction_points, (((1,), (1,)), ((), ())), precision=highest, preferred_element_type=jnp.float32)

    return lax.map(decode_one, interacted)


def reference(amplitudes, valence_points, conduction_points, screened, valence_energy, conduction_energy):
    energy = conduction_energy[None, :] - valence_energy[:, None]
    kernel_one = apply_kernel(amplitudes, valence_points, conduction_points, screened)
    first_step = 0.5 * (kernel_one + (energy - center_shift) * amplitudes)
    kernel_two = apply_kernel(first_step, valence_points, conduction_points, screened)
    return (kernel_two + (energy - center_shift) * first_step) - amplitudes
```

```python
import functools

import jax
import jax.numpy as jnp
from jax import lax
from jax.experimental import pallas as pl
from jax.experimental.pallas import tpu as pltpu
from jax.sharding import PartitionSpec as P

center_shift = 2.5
f32, bf16 = jnp.float32, jnp.bfloat16
plain = (((1,), (0,)), ((), ()))
across = (((1,), (1,)), ((), ()))
anywhere = pl.BlockSpec(memory_space=pl.ANY)
vmem_bytes = 56 * 2**20
chunks = 4


def params():
    return pltpu.CompilerParams(vmem_limit_bytes=vmem_bytes)


def cost(flops, nbytes):
    return pl.CostEstimate(flops=flops // 16, bytes_accessed=nbytes // 16, transcendentals=0)


def split(x):
    hi = x.astype(bf16)
    return hi, (x - hi.astype(f32)).astype(bf16)


def dot(a, b, dims=plain):
    return lax.dot_general(a, b, dims, preferred_element_type=f32)


def part_of(batch, rows):
    return max(k for k in range(1, batch + 1) if batch % k == 0 and (k == 1 or k * rows <= 512))


def call(kernel, name, grid, in_specs, out_specs, out_shape, scratch, estimate, args, after):
    count = len(args)

    def run(*refs):
        kernel(*refs[:count], *refs[count + len(after) :])

    return pl.pallas_call(
        run,
        grid_spec=pltpu.PrefetchScalarGridSpec(
            num_scalar_prefetch=1,
            grid=grid,
            in_specs=in_specs + [anywhere] * len(after),
            out_specs=out_specs,
            scratch_shapes=scratch,
        ),
        out_shape=out_shape,
        compiler_params=params(),
        cost_estimate=estimate,
        name=name,
    )(*args, *after)


def encode_own_kernel(part, at_ref, x_ref, c_ref, v_ref, o_ref, xs, cs, whole):
    batch, vrows, cwidth = x_ref.shape
    width = o_ref.shape[3]

    @pl.when(pl.program_id(0) == 0)
    def _():
        hi, lo = split(c_ref[...])
        cs[0:cwidth] = hi
        cs[cwidth : 2 * cwidth] = lo
        cs[2 * cwidth :] = hi

    hi, lo = split(x_ref[...].reshape(batch * vrows, cwidth))
    xs[:, 0:cwidth] = hi
    xs[:, cwidth : 2 * cwidth] = hi
    xs[:, 2 * cwidth :] = lo
    v = v_ref[...]
    for i in range(batch // part):
        prod = dot(xs[i * part * vrows : (i + 1) * part * vrows, :], cs[...])
        prod = prod.reshape(part, vrows, v.shape[1]) * v[None]
        whole[i * part : (i + 1) * part, :] = jnp.sum(prod, axis=1)
    for j in range(2):
        o_ref[j, 0] = whole[:, pl.ds(pl.multiple_of((at_ref[1] ^ j) * width, width), width)]


def encode_own(x, c, v, at, start, count, size, after):
    vrows, cwidth = x.shape[1:]
    points = c.shape[1]
    width = points // 2
    return call(
        functools.partial(encode_own_kernel, part_of(size, vrows)),
        "encode_own",
        (count,),
        [
            pl.BlockSpec((size, vrows, cwidth), lambda i, at: ((start + i) ^ at[0], 0, 0)),
            pl.BlockSpec((cwidth, points), lambda i, at: (0, 0)),
            pl.BlockSpec((vrows, points), lambda i, at: (0, 0)),
        ],
        pl.BlockSpec((2, 1, size, width), lambda i, at: (0, i, 0, 0)),
        jax.ShapeDtypeStruct((2, count, size, width), f32),
        [
            pltpu.VMEM((size * vrows, 3 * cwidth), bf16),
            pltpu.VMEM((3 * cwidth, points), bf16),
            pltpu.VMEM((size, points), f32),
        ],
        cost(6 * size * count * vrows * cwidth * points, 4 * size * count * vrows * cwidth),
        (at, x, c, v),
        after,
    )


def encode_all_kernel(part, at_ref, x_ref, hi_ref, lo_ref, v_ref, o_ref, xs):
    del at_ref
    batch, vrows, cwidth = x_ref.shape

    @pl.when((pl.program_id(0) == 0) & (pl.program_id(1) == 0))
    def _():
        hi, lo = split(x_ref[...].reshape(batch * vrows, cwidth))
        xs[:, 0:cwidth] = hi
        xs[:, cwidth : 2 * cwidth] = hi
        xs[:, 2 * cwidth :] = lo

    chi = hi_ref[0]
    w = jnp.concatenate([chi, lo_ref[0], chi], axis=0)
    v = v_ref[0]
    for i in range(batch // part):
        prod = dot(xs[i * part * vrows : (i + 1) * part * vrows, :], w)
        prod = prod.reshape(part, vrows, v.shape[1]) * v[None]
        o_ref[0, 0, i * part : (i + 1) * part, :] = jnp.sum(prod, axis=1)


def slot_of(d, n):
    return group_of(d) + ((d // 2) % 2) * (n // 2)


def group_of(d):
    return (d // 4) * 2 + d % 2


def encode_all(x, chi, clo, v, at, which, n, no, after):
    batch, vrows, cwidth = x.shape
    width = chi.shape[2] // 2
    per = n // no

    def piece(e, c, at):
        return (slot_of(((at[3] ^ e) * per + c) ^ at[2], n), 0, which ^ at[1])

    return call(
        functools.partial(encode_all_kernel, part_of(batch, vrows)),
        "encode_all",
        (no, per),
        [
            pl.BlockSpec((batch, vrows, cwidth), lambda e, c, at: (0, 0, 0)),
            pl.BlockSpec((1, cwidth, width), piece),
            pl.BlockSpec((1, cwidth, width), piece),
            pl.BlockSpec((1, vrows, width), piece),
        ],
        pl.BlockSpec((1, 1, batch, width), lambda e, c, at: (e, c, 0, 0)),
        jax.ShapeDtypeStruct((no, per, batch, width), f32),
        [pltpu.VMEM((batch * vrows, 3 * cwidth), bf16)],
        cost(6 * batch * vrows * cwidth * width * n, 4 * (cwidth + vrows) * width * n),
        (at, x, chi, clo, v),
        after,
    )


def interact_kernel(order, at_ref, e_ref, s_ref, o_ref, whole, es):
    n, per, size, width = e_ref.shape
    batch = whole.shape[0]

    @pl.when(pl.program_id(0) == 0)
    def _():
        for i, d in enumerate(order):
            row = group_of(d) * size
            for c in range(per):
                column = (2 * c + (at_ref[1] ^ ((d // 2) % 2))) * width
                whole[row : row + size, pl.ds(pl.multiple_of(column, width), width)] = e_ref[i, c]
        hi, lo = split(whole[...])
        es[0:batch] = hi
        es[batch:] = lo

    hi, lo = split(s_ref[...])
    both = dot(es[...], hi, across)
    result = both[:batch] + both[batch:] + dot(es[0:batch], lo, across)
    for g in range(batch // size):
        o_ref[0, g] = result[g * size : (g + 1) * size]


def interact(e, s, at, after):
    n, per, size, width = e.shape
    rows, columns = s.shape
    batch = n // 2 * size
    no = n // per
    tile = rows // no
    return call(
        functools.partial(interact_kernel, slots(spread_bits(n))),
        "interact",
        (no,),
        [
            pl.BlockSpec(e.shape, lambda i, at: (0, 0, 0, 0)),
            pl.BlockSpec((tile, columns), lambda i, at: (i ^ at[3], 0)),
        ],
        pl.BlockSpec((1, n // 2, size, tile), lambda i, at: (i, 0, 0, 0)),
        jax.ShapeDtypeStruct((no, n // 2, size, tile), f32),
        [pltpu.VMEM((batch, columns), f32), pltpu.VMEM((2 * batch, columns), bf16)],
        cost(6 * batch * columns * rows, 4 * columns * rows),
        (at, e, s),
        after,
    )


def decode_kernel(part, start, factor, at_ref, y_ref, hi_ref, lo_ref, v_ref, ve_ref, ce_ref, *refs):
    block_ref, o_ref, whole = refs[0], refs[-2], refs[-1]
    batch, vrows, cwidth = o_ref.shape
    tiles, tile = y_ref.shape[0], y_ref.shape[3]

    @pl.when(pl.program_id(0) == 0)
    def _():
        o_ref[...] = jnp.zeros_like(o_ref)

    for e in range(tiles):
        if tiles == 1:
            whole[...] = y_ref[e, 0]
        else:
            whole[:, pl.ds(pl.multiple_of((e ^ at_ref[3]) * tile, tile), tile)] = y_ref[e, 0]
    v = v_ref[0]
    chi, clo = hi_ref[0], lo_ref[0]
    for i in range(batch // part):
        y = whole[start + i * part : start + (i + 1) * part, :]
        weighted = (y[:, None, :] * v[None]).reshape(part * vrows, v.shape[1])
        hi, lo = split(weighted)
        got = dot(hi, chi, across) + dot(hi, clo, across) + dot(lo, chi, across)
        o_ref[i * part : (i + 1) * part] += got.reshape(part, vrows, cwidth)

    @pl.when(pl.program_id(0) == pl.num_programs(0) - 1)
    def _():
        shifted = (ce_ref[...] - ve_ref[...]) - center_shift
        result = factor * (o_ref[...] + shifted[None] * block_ref[...])
        if len(refs) > 3:
            result = result - refs[1][...]
        o_ref[...] = result


def decode(y, chi, clo, v, ve, ce, at, amplitudes, first, chunk, chunks, factor, after):
    tiles, pieces, size, tile = y.shape
    points = tiles * tile
    batch = size // chunks
    vrows, cwidth = v.shape[1], chi.shape[1]
    own = pl.BlockSpec((batch, vrows, cwidth), lambda p, at: (at[0] * chunks + chunk, 0, at[1]))
    mine = pl.BlockSpec((batch, vrows, cwidth), lambda p, at: (chunk, 0, 0))
    blocks = [amplitudes] if first is None else [first, amplitudes]
    return call(
        functools.partial(decode_kernel, part_of(batch, vrows), chunk * batch, factor),
        "decode",
        (pieces,),
        [
            pl.BlockSpec((tiles, 1, size, tile), lambda p, at: (0, p, 0, 0)),
            pl.BlockSpec((1, cwidth, points), lambda p, at: (p, 0, 0)),
            pl.BlockSpec((1, cwidth, points), lambda p, at: (p, 0, 0)),
            pl.BlockSpec((1, vrows, points), lambda p, at: (p, 0, 0)),
            pl.BlockSpec((vrows, 1), lambda p, at: (0, 0)),
            pl.BlockSpec((1, cwidth), lambda p, at: (0, at[1])),
        ]
        + ([own] if first is None else [mine, own]),
        pl.BlockSpec((batch, vrows, cwidth), lambda p, at: (0, 0, 0)),
        jax.ShapeDtypeStruct((batch, vrows, cwidth), f32),
        [pltpu.VMEM((size, points), f32)],
        cost(6 * batch * vrows * cwidth * points * pieces, 4 * (cwidth + vrows) * points * pieces),
        (at, y, chi, clo, v, ve, ce, *blocks),
        after,
    )


def place_kernel(c_ref, v_ref, *refs):
    hi_ref, lo_ref, o_ref = refs[-3:]
    hi, lo = split(c_ref[...])
    hi_ref[0] = hi
    lo_ref[0] = lo
    o_ref[0] = v_ref[...]


def place(piece, vpiece, slot, so_far, n):
    cwidth, points = piece.shape
    vrows = vpiece.shape[0]
    tile = min(points, 512)
    carried = [] if so_far is None else list(so_far)
    rows = [cwidth, cwidth, vrows]
    return pl.pallas_call(
        place_kernel,
        grid=(points // tile,),
        in_specs=[pl.BlockSpec((r, tile), lambda j: (0, j)) for r in rows[1:]]
        + [anywhere] * len(carried),
        out_specs=[pl.BlockSpec((1, r, tile), lambda j: (slot, 0, j)) for r in rows],
        out_shape=[
            jax.ShapeDtypeStruct((n, r, points), t) for r, t in zip(rows, (bf16, bf16, f32))
        ],
        input_output_aliases={2 + i: i for i in range(len(carried))},
        compiler_params=params(),
        cost_estimate=cost(0, 8 * (cwidth + vrows) * points),
        name="place",
    )(piece, vpiece, *carried)


def put_kernel(owners, chunk, chunks, count, at_ref, *refs):
    pieces, out, held, came, went = refs[:count], refs[-4], refs[-3], refs[-2], refs[-1]
    batch, _, cwidth = pieces[0].shape
    arriving = [pltpu.make_async_copy(pieces[i], held.at[i], came.at[i]) for i in range(count)]
    for copy in arriving:
        copy.start()
    leaving = []
    for i, d in enumerate(owners):
        team, half = at_ref[0] ^ group_of(d), at_ref[1] ^ ((d // 2) % 2)
        where = out.at[
            pl.ds((team * chunks + chunk) * batch, batch),
            :,
            pl.ds(pl.multiple_of(half * cwidth, cwidth), cwidth),
        ]
        arriving[i].wait()
        leaving.append(pltpu.make_async_copy(held.at[i], where, went.at[i]))
        leaving[i].start()
    for copy in leaving:
        copy.wait()


def put(pieces, chunk, chunks, at, so_far, shape):
    owners = sorted(pieces)
    count = len(owners)
    carried = [] if so_far is None else [so_far]
    block = pieces[owners[0]].shape
    return pl.pallas_call(
        functools.partial(put_kernel, owners, chunk, chunks, count),
        in_specs=[pl.BlockSpec(memory_space=pltpu.SMEM)] + [anywhere] * (count + len(carried)),
        out_specs=anywhere,
        out_shape=jax.ShapeDtypeStruct(shape, f32),
        scratch_shapes=[
            pltpu.VMEM((count,) + block, f32),
            pltpu.SemaphoreType.DMA((count,)),
            pltpu.SemaphoreType.DMA((count,)),
        ],
        input_output_aliases={count + 1 + i: i for i in range(len(carried))},
        compiler_params=params(),
        cost_estimate=cost(0, 8 * count * pieces[owners[0]].size),
        name="put",
    )(at, *[pieces[d] for d in owners], *carried)


def flip(x, axis, bit, size):
    return lax.ppermute(x, axis, [(i, i ^ bit) for i in range(size)])


def bits_of(size):
    return [1 << i for i in range(size.bit_length() - 1)]


def reorder(x, dim, by):
    for bit in bits_of(x.shape[dim]):
        shape = x.shape[:dim] + (x.shape[dim] // (2 * bit), 2, bit) + x.shape[dim + 1 :]
        swapped = lax.rev(x.reshape(shape), (dim + 1,)).reshape(x.shape)
        x = jnp.where((by // bit) % 2 == 1, swapped, x)
    return x


def tie(x, after):
    return lax.optimization_barrier((x, after))[0]


def take_bit(x, dim, bit, value):
    shape = x.shape[:dim] + (x.shape[dim] // (2 * bit), 2, bit) + x.shape[dim + 1 :]
    part = lax.index_in_dim(x.reshape(shape), value, dim + 1, keepdims=False)
    return part.reshape(x.shape[:dim] + (x.shape[dim] // 2,) + x.shape[dim + 1 :])


def scatter_sum(x, axis, size):
    for bit in reversed(bits_of(size)):
        sent = flip(x[bit:], axis, bit, size)
        x = x[:bit] + sent
    return x[0]


def collect(x, axis, size, order):
    x = x[None]
    got = {0: x[0]}
    done = []
    for bit in order:
        for d in list(got):
            got[d | bit] = flip(got[d], axis, bit, size)
        done.append(bit)
    return [got[d] for d in range(size)]


class Comm:
    def __init__(self, n, no):
        self.n, self.no = n, no
        self.me, self.mo = lax.axis_index("pts"), lax.axis_index("orb")
        self.half = (self.me // 2) % 2
        self.member = group_of(self.me)
        self.per = n // no


def slots(order):
    found = [0]
    for bit in order:
        found = found + [d | bit for d in found]
    return found


def spread_bits(n):
    return [2] + [b for b in bits_of(n) if b >= 4] + [1]


def spread_encoded(x, comm):
    x = x[None]
    for bit in spread_bits(comm.n):
        x = jnp.concatenate([x, flip(x, "pts", bit, comm.n)], axis=0)
    return x


def send_encoded_own(x, comm):
    n, no, per = comm.n, comm.no, comm.per
    x = x[None]
    for bit in bits_of(n):
        dim = 1 if bit == 2 else 2
        other = flip(take_bit(x, dim, 1, 1), "pts", bit, n)
        x = jnp.concatenate([take_bit(x, dim, 1, 0), other], axis=0)
    x = x[:, 0, 0].reshape((no, per) + x.shape[3:])
    x = reorder(x, 0, (comm.me // per) ^ comm.mo)
    if per > 1:
        x = reorder(x, 1, comm.me % per)
    return spread_encoded(scatter_sum(x, "orb", no), comm)


def send_encoded_all(send, keep, comm):
    x = keep + flip(send, "pts", 2, comm.n)
    return spread_encoded(scatter_sum(x, "orb", comm.no), comm)


def send_interacted(x, comm):
    n, no = comm.n, comm.no
    x = x[:, None]
    for bit in [b for b in bits_of(n) if b != 2]:
        other = flip(take_bit(x, 2, 1, 1), "pts", bit, n)
        x = jnp.concatenate([take_bit(x, 2, 1, 0), other], axis=1)
    x = scatter_sum(x[:, :, 0], "orb", no)[None]
    for bit in bits_of(no):
        x = jnp.concatenate([x, flip(x, "orb", bit, no)], axis=0)
    x = jnp.concatenate([x, flip(x, "pts", 2, n)], axis=1)
    if x.shape[3] % 128 == 0:
        return x
    x = reorder(x, 0, comm.mo).transpose(1, 2, 0, 3)
    return x.reshape((1,) + x.shape[:2] + (-1,))


def around(x, order, n):
    got = {0: x}
    stages = []
    for bit in order:
        new = {d | bit: flip(got[d], "pts", bit, n) for d in list(got)}
        got.update(new)
        stages.append(new)
    return got, stages


def body(
    amplitudes, valence_points, conduction_points, screened, valence_energy, conduction_energy, n, no
):
    comm = Comm(n, no)
    ve, ce = valence_energy[:, None], conduction_energy[None, :]
    teams = n // 2
    size = amplitudes.shape[0] // teams
    at = jnp.stack([comm.member, comm.half, comm.me, comm.mo]).astype(jnp.int32)

    cwidth = conduction_points.shape[0] // 2
    mine = lax.dynamic_slice_in_dim(conduction_points, comm.half * cwidth, cwidth, 0)
    other = lax.dynamic_slice_in_dim(conduction_points, (1 - comm.half) * cwidth, cwidth, 0)
    high = [b for b in bits_of(n) if b >= 4]

    pieces = {0: mine, 2: flip(other, "pts", 2, n)}
    vpieces = {0: valence_points, high[0]: flip(valence_points, "pts", high[0], n)}
    pieces[high[0]] = flip(mine, "pts", high[0], n)
    early = (pieces[2], pieces[high[0]])
    parts, after = [], ()
    runs = 4 if teams % 4 == 0 else 1
    for i in range(runs):
        part = encode_own(
            amplitudes,
            conduction_points,
            valence_points,
            at,
            i * (teams // runs),
            teams // runs,
            size,
            after + (early if i == runs - 1 else ()),
        )
        after = (part,)
        parts.append(part)
    part = jnp.concatenate(parts, axis=1)
    for bit in high:
        for d in list(pieces):
            if d | bit not in pieces:
                pieces[d | bit] = flip(pieces[d], "pts", bit, n)
    for bit in high[1:] + [2]:
        for d in list(vpieces):
            vpieces[d | bit] = flip(vpieces[d], "pts", bit, n)
    second = tuple(pieces[d] for d in pieces if d not in (0, 2, high[0]))
    second += tuple(vpieces[d] for d in vpieces if d != 0)
    e = send_encoded_own(part, comm)
    got = interact(e, screened, at, after + second)

    for d in list(pieces):
        pieces[d | 1] = flip(pieces[d], "pts", 1, n)
        vpieces[d | 1] = flip(vpieces[d], "pts", 1, n)
    placed = None
    for d in pieces:
        placed = place(pieces[d], vpieces[d], slot_of(d, n), placed, n)
    chi, clo, v = placed

    def decoded(y, first, chunk, chunks, factor, after):
        return decode(y, chi, clo, v, ve, ce, at, amplitudes, first, chunk, chunks, factor, after)

    y = send_interacted(got, comm)
    first = decoded(y, None, 0, 1, 0.5, ())
    send = encode_all(first, chi, clo, v, at, 1, n, no, ())
    keep = encode_all(first, chi, clo, v, at, 0, n, no, (send,))
    e = send_encoded_all(send, keep, comm)
    y = send_interacted(interact(e, screened, at, ()), comm)
    out, after = None, ()
    waiting = []
    for chunk in range(chunks):
        if chunk >= 2:
            after += tuple(waiting[chunk - 2][1][0].values())
        if chunk >= 3:
            after += tuple(waiting[chunk - 3][1][-1].values())
        got = decoded(y, first, chunk, chunks, 1.0, after)
        after = (got,)
        waiting.append(around(got, [2] + high if chunk % 2 == 0 else high + [2], n))
    for chunk, (near, _) in enumerate(waiting):
        out = put(near, chunk, chunks, at, out, amplitudes.shape)
        far = {d | 1: flip(near[d], "pts", 1, n) for d in near}
        out = put(far, chunk, chunks, at, out, amplitudes.shape)
    return out


def solution(mesh):
    n, no = mesh.shape["pts"], mesh.shape["orb"]
    return jax.shard_map(
        functools.partial(body, n=n, no=no),
        mesh=mesh,
        in_specs=(
            P(None, "orb", None),
            P("orb", "pts"),
            P(None, "pts"),
            P("pts", "orb"),
            P("orb"),
            P(),
        ),
        out_specs=P(None, "orb", None),
        check_vma=False,
    )
```

```python
import functools

import jax
import jax.numpy as jnp
from jax import lax
from jax.experimental import pallas as pl
from jax.experimental.pallas import tpu as pltpu
from jax.sharding import PartitionSpec as P

center_shift = 2.5
f32, bf16 = jnp.float32, jnp.bfloat16
plain = (((1,), (0,)), ((), ()))
across = (((1,), (1,)), ((), ()))
anywhere = pl.BlockSpec(memory_space=pl.ANY)
vmem_bytes = 56 * 2**20
chunks = 4


def params():
    return pltpu.CompilerParams(vmem_limit_bytes=vmem_bytes)


def cost(flops, nbytes):
    return pl.CostEstimate(flops=flops, bytes_accessed=nbytes, transcendentals=0)


def split(x):
    hi = x.astype(bf16)
    return hi, (x - hi.astype(f32)).astype(bf16)


def dot(a, b, dims=plain):
    return lax.dot_general(a, b, dims, preferred_element_type=f32)


def part_of(batch, rows):
    return max(k for k in range(1, batch + 1) if batch % k == 0 and (k == 1 or k * rows <= 512))


def call(kernel, name, grid, in_specs, out_specs, out_shape, scratch, estimate, args, after):
    count = len(args)

    def run(*refs):
        kernel(*refs[:count], *refs[count + len(after) :])

    return pl.pallas_call(
        run,
        grid_spec=pltpu.PrefetchScalarGridSpec(
            num_scalar_prefetch=1,
            grid=grid,
            in_specs=in_specs + [anywhere] * len(after),
            out_specs=out_specs,
            scratch_shapes=scratch,
        ),
        out_shape=out_shape,
        compiler_params=params(),
        cost_estimate=estimate,
        name=name,
    )(*args, *after)


def encode_own_kernel(part, at_ref, x_ref, c_ref, v_ref, o_ref, xs, cs, whole):
    batch, vrows, cwidth = x_ref.shape
    width = o_ref.shape[3]

    @pl.when(pl.program_id(0) == 0)
    def _():
        hi, lo = split(c_ref[...])
        cs[0:cwidth] = hi
        cs[cwidth : 2 * cwidth] = lo
        cs[2 * cwidth :] = hi

    hi, lo = split(x_ref[...].reshape(batch * vrows, cwidth))
    xs[:, 0:cwidth] = hi
    xs[:, cwidth : 2 * cwidth] = hi
    xs[:, 2 * cwidth :] = lo
    v = v_ref[...]
    for i in range(batch // part):
        prod = dot(xs[i * part * vrows : (i + 1) * part * vrows, :], cs[...])
        prod = prod.reshape(part, vrows, v.shape[1]) * v[None]
        whole[i * part : (i + 1) * part, :] = jnp.sum(prod, axis=1)
    for j in range(2):
        o_ref[j, 0] = whole[:, pl.ds(pl.multiple_of((at_ref[1] ^ j) * width, width), width)]


def encode_own(x, c, v, at, start, count, size, after):
    vrows, cwidth = x.shape[1:]
    points = c.shape[1]
    width = points // 2
    return call(
        functools.partial(encode_own_kernel, part_of(size, vrows)),
        "encode_own",
        (count,),
        [
            pl.BlockSpec((size, vrows, cwidth), lambda i, at: ((start + i) ^ at[0], 0, 0)),
            pl.BlockSpec((cwidth, points), lambda i, at: (0, 0)),
            pl.BlockSpec((vrows, points), lambda i, at: (0, 0)),
        ],
        pl.BlockSpec((2, 1, size, width), lambda i, at: (0, i, 0, 0)),
        jax.ShapeDtypeStruct((2, count, size, width), f32),
        [
            pltpu.VMEM((size * vrows, 3 * cwidth), bf16),
            pltpu.VMEM((3 * cwidth, points), bf16),
            pltpu.VMEM((size, points), f32),
        ],
        cost(size * count * vrows * cwidth * points // 4, size * count * vrows * cwidth // 4),
        (at, x, c, v),
        after,
    )


def encode_all_kernel(part, at_ref, x_ref, hi_ref, lo_ref, v_ref, o_ref, xs):
    del at_ref
    batch, vrows, cwidth = x_ref.shape

    @pl.when((pl.program_id(0) == 0) & (pl.program_id(1) == 0))
    def _():
        hi, lo = split(x_ref[...].reshape(batch * vrows, cwidth))
        xs[:, 0:cwidth] = hi
        xs[:, cwidth : 2 * cwidth] = hi
        xs[:, 2 * cwidth :] = lo

    chi = hi_ref[0]
    w = jnp.concatenate([chi, lo_ref[0], chi], axis=0)
    v = v_ref[0]
    for i in range(batch // part):
        prod = dot(xs[i * part * vrows : (i + 1) * part * vrows, :], w)
        prod = prod.reshape(part, vrows, v.shape[1]) * v[None]
        o_ref[0, 0, i * part : (i + 1) * part, :] = jnp.sum(prod, axis=1)


def slot_of(d, n):
    return group_of(d) + ((d // 2) % 2) * (n // 2)


def group_of(d):
    return (d // 4) * 2 + d % 2


def encode_all(x, chi, clo, v, at, which, n, no, after):
    batch, vrows, cwidth = x.shape
    width = chi.shape[2] // 2
    per = n // no

    def piece(e, c, at):
        return (slot_of(((at[3] ^ e) * per + c) ^ at[2], n), 0, which ^ at[1])

    return call(
        functools.partial(encode_all_kernel, part_of(batch, vrows)),
        "encode_all",
        (no, per),
        [
            pl.BlockSpec((batch, vrows, cwidth), lambda e, c, at: (0, 0, 0)),
            pl.BlockSpec((1, cwidth, width), piece),
            pl.BlockSpec((1, cwidth, width), piece),
            pl.BlockSpec((1, vrows, width), piece),
        ],
        pl.BlockSpec((1, 1, batch, width), lambda e, c, at: (e, c, 0, 0)),
        jax.ShapeDtypeStruct((no, per, batch, width), f32),
        [pltpu.VMEM((batch * vrows, 3 * cwidth), bf16)],
        cost(6 * batch * vrows * cwidth * width * n, 4 * (cwidth + vrows) * width * n),
        (at, x, chi, clo, v),
        after,
    )


def interact_kernel(order, at_ref, e_ref, s_ref, o_ref, whole, es):
    n, per, size, width = e_ref.shape
    batch = whole.shape[0]

    @pl.when(pl.program_id(0) == 0)
    def _():
        for i, d in enumerate(order):
            row = group_of(d) * size
            for c in range(per):
                column = (2 * c + (at_ref[1] ^ ((d // 2) % 2))) * width
                whole[row : row + size, pl.ds(pl.multiple_of(column, width), width)] = e_ref[i, c]
        hi, lo = split(whole[...])
        es[0:batch] = hi
        es[batch:] = lo

    hi, lo = split(s_ref[...])
    both = dot(es[...], hi, across)
    result = both[:batch] + both[batch:] + dot(es[0:batch], lo, across)
    for g in range(batch // size):
        o_ref[0, g] = result[g * size : (g + 1) * size]


def interact(e, s, at, after):
    n, per, size, width = e.shape
    rows, columns = s.shape
    batch = n // 2 * size
    no = n // per
    tile = rows // no
    return call(
        functools.partial(interact_kernel, slots(spread_bits(n))),
        "interact",
        (no,),
        [
            pl.BlockSpec(e.shape, lambda i, at: (0, 0, 0, 0)),
            pl.BlockSpec((tile, columns), lambda i, at: (i ^ at[3], 0)),
        ],
        pl.BlockSpec((1, n // 2, size, tile), lambda i, at: (i, 0, 0, 0)),
        jax.ShapeDtypeStruct((no, n // 2, size, tile), f32),
        [pltpu.VMEM((batch, columns), f32), pltpu.VMEM((2 * batch, columns), bf16)],
        cost(6 * batch * columns * rows, 4 * columns * rows),
        (at, e, s),
        after,
    )


def decode_kernel(part, start, factor, stage, at_ref, y_ref, hi_ref, lo_ref, v_ref, ve_ref, ce_ref, *refs):
    o_ref, whole = refs[-2:]
    batch, vrows, cwidth = o_ref.shape
    tiles, tile = y_ref.shape[0], y_ref.shape[3]

    @pl.when(pl.program_id(0) == 0)
    def _():
        o_ref[...] = refs[0][...] if stage else jnp.zeros_like(o_ref)

    for e in range(tiles):
        if tiles == 1:
            whole[...] = y_ref[e, 0]
        else:
            whole[:, pl.ds(pl.multiple_of((e ^ at_ref[3]) * tile, tile), tile)] = y_ref[e, 0]
    v = v_ref[0]
    chi, clo = hi_ref[0], lo_ref[0]
    for i in range(batch // part):
        y = whole[start + i * part : start + (i + 1) * part, :]
        weighted = (y[:, None, :] * v[None]).reshape(part * vrows, v.shape[1])
        hi, lo = split(weighted)
        got = dot(hi, chi, across) + dot(hi, clo, across) + dot(lo, chi, across)
        o_ref[i * part : (i + 1) * part] += got.reshape(part, vrows, cwidth)

    if factor is not None:

        @pl.when(pl.program_id(0) == pl.num_programs(0) - 1)
        def _():
            shifted = (ce_ref[...] - ve_ref[...]) - center_shift
            result = factor * (o_ref[...] + shifted[None] * refs[stage][...])
            if len(refs) > 3 + stage:
                result = result - refs[stage + 1][...]
            o_ref[...] = result


def decode(y, chi, clo, v, ve, ce, at, amplitudes, first, chunk, chunks, factor, after):
    tiles, pieces, size, tile = y[0].shape
    points = tiles * tile
    batch = size // chunks
    vrows, cwidth = v.shape[1], chi.shape[1]
    own = pl.BlockSpec((batch, vrows, cwidth), lambda p, at: (at[0] * chunks + chunk, 0, at[1]))
    mine = pl.BlockSpec((batch, vrows, cwidth), lambda p, at: (chunk, 0, 0))
    fixed = pl.BlockSpec((batch, vrows, cwidth), lambda p, at: (0, 0, 0))
    blocks = [amplitudes] if first is None else [first, amplitudes]
    total = None
    for stage in range(len(y)):
        last = stage == len(y) - 1

        def piece(p, at, stage=stage):
            return (stage * pieces + p, 0, 0)

        total = call(
            functools.partial(
                decode_kernel, part_of(batch, vrows), chunk * batch, factor if last else None, stage
            ),
            "decode",
            (pieces,),
            [
                pl.BlockSpec((tiles, 1, size, tile), lambda p, at: (0, p, 0, 0)),
                pl.BlockSpec((1, cwidth, points), piece),
                pl.BlockSpec((1, cwidth, points), piece),
                pl.BlockSpec((1, vrows, points), piece),
                pl.BlockSpec((vrows, 1), lambda p, at: (0, 0)),
                pl.BlockSpec((1, cwidth), lambda p, at: (0, at[1])),
            ]
            + [fixed] * stage
            + (([own] if first is None else [mine, own]) if last else []),
            fixed,
            jax.ShapeDtypeStruct((batch, vrows, cwidth), f32),
            [pltpu.VMEM((size, points), f32)],
            cost(6 * batch * vrows * cwidth * points * pieces, 4 * (cwidth + vrows) * points * pieces),
            (at, y[stage], chi, clo, v, ve, ce, *([total] * stage), *(blocks if last else [])),
            after,
        )
        after = ()
    return total


def place_kernel(c_ref, *refs):
    hi_ref, lo_ref, mark_ref = refs[-3:]
    hi, lo = split(c_ref[...])
    hi_ref[0] = hi
    lo_ref[0] = lo
    mark_ref[...] = jnp.zeros_like(mark_ref)


def place(piece, slot, so_far, n):
    cwidth, points = piece.shape
    tile = min(points, 1024)
    carried = [] if so_far is None else list(so_far)
    shape = jax.ShapeDtypeStruct((n, cwidth, points), bf16)
    out = pl.BlockSpec((1, cwidth, tile), lambda j: (slot, 0, j))
    *placed, mark = pl.pallas_call(
        place_kernel,
        grid=(points // tile,),
        in_specs=[pl.BlockSpec((cwidth, tile), lambda j: (0, j))] + [anywhere] * len(carried),
        out_specs=[out, out, pl.BlockSpec((8, 128), lambda j: (0, 0))],
        out_shape=[shape, shape, jax.ShapeDtypeStruct((8, 128), f32)],
        input_output_aliases={1 + i: i for i in range(len(carried))},
        compiler_params=params(),
        cost_estimate=cost(0, 16 * cwidth * points),
        name="place",
    )(piece, *carried)
    return placed, mark


def put_kernel(owners, chunk, chunks, count, at_ref, *refs):
    pieces, (out, mark, held, came, went) = refs[:count], refs[-5:]
    mark[...] = jnp.zeros_like(mark)
    batch, _, cwidth = pieces[0].shape
    arriving = [pltpu.make_async_copy(pieces[i], held.at[i], came.at[i]) for i in range(count)]
    for copy in arriving:
        copy.start()
    leaving = []
    for i, d in enumerate(owners):
        team, half = at_ref[0] ^ group_of(d), at_ref[1] ^ ((d // 2) % 2)
        where = out.at[
            pl.ds((team * chunks + chunk) * batch, batch),
            :,
            pl.ds(pl.multiple_of(half * cwidth, cwidth), cwidth),
        ]
        arriving[i].wait()
        leaving.append(pltpu.make_async_copy(held.at[i], where, went.at[i]))
        leaving[i].start()
    for copy in leaving:
        copy.wait()


def put(pieces, chunk, chunks, at, so_far, shape):
    owners = sorted(pieces)
    count = len(owners)
    carried = [] if so_far is None else [so_far]
    block = pieces[owners[0]].shape
    return pl.pallas_call(
        functools.partial(put_kernel, owners, chunk, chunks, count),
        in_specs=[pl.BlockSpec(memory_space=pltpu.SMEM)] + [anywhere] * (count + len(carried)),
        out_specs=[anywhere, pl.BlockSpec(memory_space=pltpu.VMEM)],
        out_shape=[jax.ShapeDtypeStruct(shape, f32), jax.ShapeDtypeStruct((8, 128), f32)],
        scratch_shapes=[
            pltpu.VMEM((count,) + block, f32),
            pltpu.SemaphoreType.DMA((count,)),
            pltpu.SemaphoreType.DMA((count,)),
        ],
        input_output_aliases={count + 1 + i: i for i in range(len(carried))},
        compiler_params=params(),
        cost_estimate=cost(0, 16 * count * pieces[owners[0]].size),
        name="put",
    )(at, *[pieces[d] for d in owners], *carried)


def flip(x, axis, bit, size):
    return lax.ppermute(x, axis, [(i, i ^ bit) for i in range(size)])


def bits_of(size):
    return [1 << i for i in range(size.bit_length() - 1)]


def reorder(x, dim, by):
    for bit in bits_of(x.shape[dim]):
        shape = x.shape[:dim] + (x.shape[dim] // (2 * bit), 2, bit) + x.shape[dim + 1 :]
        swapped = lax.rev(x.reshape(shape), (dim + 1,)).reshape(x.shape)
        x = jnp.where((by // bit) % 2 == 1, swapped, x)
    return x


def tie(x, after):
    return lax.optimization_barrier((x, after))[0]


def take_bit(x, dim, bit, value):
    shape = x.shape[:dim] + (x.shape[dim] // (2 * bit), 2, bit) + x.shape[dim + 1 :]
    part = lax.index_in_dim(x.reshape(shape), value, dim + 1, keepdims=False)
    return part.reshape(x.shape[:dim] + (x.shape[dim] // 2,) + x.shape[dim + 1 :])


def scatter_sum(x, axis, size):
    for bit in bits_of(size):
        x = take_bit(x, 0, 1, 0) + flip(take_bit(x, 0, 1, 1), axis, bit, size)
    return x[0]


class Comm:
    def __init__(self, n, no):
        self.n, self.no = n, no
        self.me, self.mo = lax.axis_index("pts"), lax.axis_index("orb")
        self.half = (self.me // 2) % 2
        self.member = group_of(self.me)
        self.per = n // no


def slots(order):
    found = [0]
    for bit in order:
        found = found + [d | bit for d in found]
    return found


def spread_bits(n):
    return [2] + [b for b in bits_of(n) if b >= 4] + [1]


def join_kernel(a_ref, b_ref, *refs):
    o_ref = refs[-1]
    o_ref[0] = a_ref[...]
    o_ref[1] = b_ref[...]


def join(a, b, after):
    whole = pl.BlockSpec(memory_space=pltpu.VMEM)
    out = pl.pallas_call(
        join_kernel,
        in_specs=[whole, whole] + [anywhere] * len(after),
        out_specs=whole,
        out_shape=jax.ShapeDtypeStruct((2,) + a.shape, f32),
        compiler_params=params(),
        cost_estimate=cost(0, 16 * a.size),
        name="join",
    )(a, b, *after)
    return out.reshape((2 * a.shape[0],) + a.shape[1:])


def spread_encoded(x, comm, after=()):
    x = x[None]
    for i, bit in enumerate(spread_bits(comm.n)):
        other = flip(x, "pts", bit, comm.n)
        x = join(x, other, after) if after and i == 0 else jnp.concatenate([x, other], axis=0)
    return x


def arrange_kernel(at_ref, x_ref, v_ref, o_ref, copy_ref):
    no, per = o_ref.shape[:2]
    for e in range(no):
        for c in range(per):
            o_ref[e, c] = x_ref[((e ^ at_ref[3]) * per + c) ^ at_ref[2]]
    copy_ref[...] = v_ref[...]


def arrange(x, v, at, no, after):
    n, batch, width = x.shape
    per = n // no
    return call(
        arrange_kernel,
        "arrange",
        (1,),
        [
            pl.BlockSpec((n, batch, width), lambda i, at: (0, 0, 0)),
            pl.BlockSpec(v.shape, lambda i, at: (0, 0)),
        ],
        [
            pl.BlockSpec((no, per, batch, width), lambda i, at: (0, 0, 0, 0)),
            pl.BlockSpec(v.shape, lambda i, at: (0, 0)),
        ],
        [jax.ShapeDtypeStruct((no, per, batch, width), f32), jax.ShapeDtypeStruct(v.shape, f32)],
        [],
        cost(0, 8 * x.size),
        (at, x, v),
        after,
    )


def send_encoded_own(x, v, at, comm, after):
    n, no = comm.n, comm.no
    x = x[None]
    for bit in bits_of(n):
        dim = 1 if bit == 2 else 2
        other = flip(take_bit(x, dim, 1, 1), "pts", bit, n)
        x = jnp.concatenate([take_bit(x, dim, 1, 0), other], axis=0)
    x, v = arrange(x[:, 0, 0], v, at, no, after)
    vpieces = {0: v}
    for bit in [b for b in bits_of(n) if b >= 4] + [2]:
        for d in list(vpieces):
            vpieces[d | bit] = flip(vpieces[d], "pts", bit, n)
    early = tuple(vpieces[b] for b in bits_of(n) if b >= 4)
    return spread_encoded(scatter_sum(x, "orb", no), comm, early), vpieces


def send_encoded_all(send, keep, comm):
    x = keep + flip(send, "pts", 2, comm.n)
    return spread_encoded(scatter_sum(x, "orb", comm.no), comm)


def send_interacted(x, comm, before=None):
    n, no = comm.n, comm.no
    x = x[:, None]
    for bit in [b for b in bits_of(n) if b != 2]:
        other = flip(take_bit(x, 2, 1, 1), "pts", bit, n)
        x = jnp.concatenate([take_bit(x, 2, 1, 0), other], axis=1)
    x = x[:, :, 0]
    if before is not None:
        x = tie(x, before)
    x = scatter_sum(x, "orb", no)[None]
    near, far = {0: x}, {0: flip(x, "pts", 2, n)}
    for bit in reversed(bits_of(no)):
        have = sorted(near)
        more = flip(jnp.concatenate([near[e] for e in have], axis=0), "orb", bit, no)
        side = flip(more, "pts", 2, n)
        for i, e in enumerate(have):
            near[e | bit], far[e | bit] = more[i : i + 1], side[i : i + 1]
    result = []
    for side in (near, far):
        x = jnp.concatenate([side[e] for e in range(no)], axis=0)
        if x.shape[3] % 128:
            x = reorder(x, 0, comm.mo).transpose(1, 2, 0, 3)
            x = x.reshape((1,) + x.shape[:2] + (-1,))
        result.append(x)
    return result


def around(x, order, n):
    got = {0: x}
    for bit in order:
        for d in list(got):
            got[d | bit] = flip(got[d], "pts", bit, n)
    return got


def body(
    amplitudes, valence_points, conduction_points, screened, valence_energy, conduction_energy, n, no
):
    comm = Comm(n, no)
    ve, ce = valence_energy[:, None], conduction_energy[None, :]
    teams = n // 2
    size = amplitudes.shape[0] // teams
    at = jnp.stack([comm.member, comm.half, comm.me, comm.mo]).astype(jnp.int32)

    cwidth = conduction_points.shape[0] // 2
    mine = lax.dynamic_slice_in_dim(conduction_points, comm.half * cwidth, cwidth, 0)
    other = lax.dynamic_slice_in_dim(conduction_points, (1 - comm.half) * cwidth, cwidth, 0)
    high = [b for b in bits_of(n) if b >= 4]


    pieces = {0: mine, 2: flip(other, "pts", 2, n), high[0]: flip(mine, "pts", high[0], n)}
    early = (pieces[2], pieces[high[0]])
    cuts = [0, teams - teams // 4, teams]
    parts, after = [], ()
    for start, end in zip(cuts, cuts[1:]):
        part = encode_own(
            amplitudes, conduction_points, valence_points, at, start, end - start, size, after
        )
        after = (part,) + early
        parts.append(part)
    for bit in high:
        for d in list(pieces):
            if d | bit not in pieces:
                pieces[d | bit] = flip(tie(pieces[d], parts[0]), "pts", bit, n)
    across_x = tuple(pieces[d] for d in pieces if d not in (0, 2, high[0]))
    near = list(pieces)
    placed, marks = None, []
    for d in near:
        placed, mark = place(pieces[d], slot_of(d, n), placed, n)
        marks.append(mark)
        pieces[d | 1] = flip(pieces[d], "pts", 1, n)
    e, vpieces = send_encoded_own(
        jnp.concatenate(parts, axis=1),
        valence_points,
        at,
        comm,
        across_x + tuple(marks[: len(marks) - len(across_x)]),
    )
    got = interact(e, screened, at, after)
    for d in near:
        placed, _ = place(pieces[d | 1], slot_of(d | 1, n), placed, n)

    for d in list(vpieces):
        vpieces[d | 1] = flip(vpieces[d], "pts", 1, n)
    v = jnp.stack([vpieces[d] for d in sorted(vpieces, key=lambda d: slot_of(d, n))])
    chi, clo = placed

    def decoded(y, first, chunk, chunks, factor, after):
        return decode(y, chi, clo, v, ve, ce, at, amplitudes, first, chunk, chunks, factor, after)

    y = send_interacted(got, comm)
    first = decoded(y, None, 0, 1, 0.5, ())
    send = encode_all(first, chi, clo, v, at, 1, n, no, ())
    keep = encode_all(first, chi, clo, v, at, 0, n, no, (send,))
    e = send_encoded_all(send, keep, comm)
    y = send_interacted(interact(e, screened, at, ()), comm)
    out, after, marks = None, (), []
    waiting, decodes = [], []
    both = [jnp.concatenate(y, axis=1)]
    for chunk in range(chunks):
        if chunk >= 2:
            after += tuple(waiting[chunk - 2][b] for b in high + [2])
        if chunk >= 3:
            after += tuple(waiting[chunk - 3].values())
        got = decoded(y if chunk == 0 else both, first, chunk, chunks, 1.0, after)
        after = (got,)
        decodes.append(got)
        waiting.append(around(got, [2] + high if chunk % 2 == 0 else high + [2], n))
    for chunk, blocks in enumerate(waiting):
        for d in list(blocks):
            block = blocks[d]
            if chunk < chunks - 2:
                block = tie(block, decodes[chunk + 2])
            if chunk == chunks - 1:
                block = tie(block, tuple(marks[: chunks - 2]))
            blocks[d | 1] = flip(block, "pts", 1, n)
        if chunk < chunks - 1:
            out, mark = put(blocks, chunk, chunks, at, out, amplitudes.shape)
            marks.append(mark)
        else:
            near = {d: blocks[d] for d in blocks if d % 2 == 0}
            out, _ = put(near, chunk, chunks, at, out, amplitudes.shape)
            far = {d: blocks[d] for d in blocks if d % 2 == 1}
            out, _ = put(far, chunk, chunks, at, out, amplitudes.shape)
    return out


def solution(mesh):
    n, no = mesh.shape["pts"], mesh.shape["orb"]
    return jax.shard_map(
        functools.partial(body, n=n, no=no),
        mesh=mesh,
        in_specs=(
            P(None, "orb", None),
            P("orb", "pts"),
            P(None, "pts"),
            P("pts", "orb"),
            P("orb"),
            P(),
        ),
        out_specs=P(None, "orb", None),
        check_vma=False,
    )
```

```python
import functools

import jax
import jax.numpy as jnp
from jax import lax
from jax.experimental import pallas as pl
from jax.experimental.pallas import tpu as pltpu
from jax.sharding import PartitionSpec as P

center_shift = 2.5
f32, bf16 = jnp.float32, jnp.bfloat16
plain = (((1,), (0,)), ((), ()))
across = (((1,), (1,)), ((), ()))
anywhere = pl.BlockSpec(memory_space=pl.ANY)
vmem_bytes = 56 * 2**20
chunks = 4


def params():
    return pltpu.CompilerParams(vmem_limit_bytes=vmem_bytes)


def cost(flops, nbytes):
    return pl.CostEstimate(flops=flops, bytes_accessed=nbytes, transcendentals=0)


def split(x):
    hi = x.astype(bf16)
    return hi, (x - hi.astype(f32)).astype(bf16)


def dot(a, b, dims=plain):
    return lax.dot_general(a, b, dims, preferred_element_type=f32)


def part_of(batch, rows):
    return max(k for k in range(1, batch + 1) if batch % k == 0 and (k == 1 or k * rows <= 512))


def call(kernel, name, grid, in_specs, out_specs, out_shape, scratch, estimate, args, after):
    count = len(args)

    def run(*refs):
        kernel(*refs[:count], *refs[count + len(after) :])

    return pl.pallas_call(
        run,
        grid_spec=pltpu.PrefetchScalarGridSpec(
            num_scalar_prefetch=1,
            grid=grid,
            in_specs=in_specs + [anywhere] * len(after),
            out_specs=out_specs,
            scratch_shapes=scratch,
        ),
        out_shape=out_shape,
        compiler_params=params(),
        cost_estimate=estimate,
        name=name,
    )(*args, *after)


def encode_own_kernel(part, at_ref, x_ref, c_ref, v_ref, o_ref, xs, cs, whole):
    batch, vrows, cwidth = x_ref.shape
    width = o_ref.shape[3]

    @pl.when(pl.program_id(0) == 0)
    def _():
        hi, lo = split(c_ref[...])
        cs[0:cwidth] = hi
        cs[cwidth : 2 * cwidth] = lo
        cs[2 * cwidth :] = hi

    hi, lo = split(x_ref[...].reshape(batch * vrows, cwidth))
    xs[:, 0:cwidth] = hi
    xs[:, cwidth : 2 * cwidth] = hi
    xs[:, 2 * cwidth :] = lo
    v = v_ref[...]
    for i in range(batch // part):
        prod = dot(xs[i * part * vrows : (i + 1) * part * vrows, :], cs[...])
        prod = prod.reshape(part, vrows, v.shape[1]) * v[None]
        whole[i * part : (i + 1) * part, :] = jnp.sum(prod, axis=1)
    for j in range(2):
        o_ref[j, 0] = whole[:, pl.ds(pl.multiple_of((at_ref[1] ^ j) * width, width), width)]


def encode_own(x, c, v, at, start, count, size, after):
    vrows, cwidth = x.shape[1:]
    points = c.shape[1]
    width = points // 2
    return call(
        functools.partial(encode_own_kernel, part_of(size, vrows)),
        "encode_own",
        (count,),
        [
            pl.BlockSpec((size, vrows, cwidth), lambda i, at: ((start + i) ^ at[0], 0, 0)),
            pl.BlockSpec((cwidth, points), lambda i, at: (0, 0)),
            pl.BlockSpec((vrows, points), lambda i, at: (0, 0)),
        ],
        pl.BlockSpec((2, 1, size, width), lambda i, at: (0, i, 0, 0)),
        jax.ShapeDtypeStruct((2, count, size, width), f32),
        [
            pltpu.VMEM((size * vrows, 3 * cwidth), bf16),
            pltpu.VMEM((3 * cwidth, points), bf16),
            pltpu.VMEM((size, points), f32),
        ],
        cost(size * count * vrows * cwidth * points // 4, size * count * vrows * cwidth // 4),
        (at, x, c, v),
        after,
    )


def encode_all_kernel(part, at_ref, x_ref, hi_ref, lo_ref, v_ref, o_ref, xs):
    del at_ref
    batch, vrows, cwidth = x_ref.shape

    @pl.when((pl.program_id(0) == 0) & (pl.program_id(1) == 0))
    def _():
        hi, lo = split(x_ref[...].reshape(batch * vrows, cwidth))
        xs[:, 0:cwidth] = hi
        xs[:, cwidth : 2 * cwidth] = hi
        xs[:, 2 * cwidth :] = lo

    chi = hi_ref[0]
    w = jnp.concatenate([chi, lo_ref[0], chi], axis=0)
    v = v_ref[0]
    for i in range(batch // part):
        prod = dot(xs[i * part * vrows : (i + 1) * part * vrows, :], w)
        prod = prod.reshape(part, vrows, v.shape[1]) * v[None]
        o_ref[0, 0, i * part : (i + 1) * part, :] = jnp.sum(prod, axis=1)


def slot_of(d, n):
    return group_of(d) + ((d // 2) % 2) * (n // 2)


def group_of(d):
    return (d // 4) * 2 + d % 2


def encode_all(x, chi, clo, v, at, which, n, no, after):
    batch, vrows, cwidth = x.shape
    width = chi.shape[2] // 2
    per = n // no

    def piece(e, c, at):
        return (slot_of(((at[3] ^ e) * per + c) ^ at[2], n), 0, which ^ at[1])

    return call(
        functools.partial(encode_all_kernel, part_of(batch, vrows)),
        "encode_all",
        (no, per),
        [
            pl.BlockSpec((batch, vrows, cwidth), lambda e, c, at: (0, 0, 0)),
            pl.BlockSpec((1, cwidth, width), piece),
            pl.BlockSpec((1, cwidth, width), piece),
            pl.BlockSpec((1, vrows, width), piece),
        ],
        pl.BlockSpec((1, 1, batch, width), lambda e, c, at: (e, c, 0, 0)),
        jax.ShapeDtypeStruct((no, per, batch, width), f32),
        [pltpu.VMEM((batch * vrows, 3 * cwidth), bf16)],
        cost(6 * batch * vrows * cwidth * width * n, 4 * (cwidth + vrows) * width * n),
        (at, x, chi, clo, v),
        after,
    )


def interact_kernel(order, at_ref, e_ref, s_ref, o_ref, whole, es):
    n, per, size, width = e_ref.shape
    batch = whole.shape[0]

    @pl.when(pl.program_id(0) == 0)
    def _():
        for i, d in enumerate(order):
            row = group_of(d) * size
            for c in range(per):
                column = (2 * c + (at_ref[1] ^ ((d // 2) % 2))) * width
                whole[row : row + size, pl.ds(pl.multiple_of(column, width), width)] = e_ref[i, c]
        hi, lo = split(whole[...])
        es[0:batch] = hi
        es[batch:] = lo

    hi, lo = split(s_ref[...])
    both = dot(es[...], hi, across)
    result = both[:batch] + both[batch:] + dot(es[0:batch], lo, across)
    for g in range(batch // size):
        o_ref[0, g] = result[g * size : (g + 1) * size]


def interact(e, s, at, after):
    n, per, size, width = e.shape
    rows, columns = s.shape
    batch = n // 2 * size
    no = n // per
    tile = rows // no
    return call(
        functools.partial(interact_kernel, slots(spread_bits(n))),
        "interact",
        (no,),
        [
            pl.BlockSpec(e.shape, lambda i, at: (0, 0, 0, 0)),
            pl.BlockSpec((tile, columns), lambda i, at: (i ^ at[3], 0)),
        ],
        pl.BlockSpec((1, n // 2, size, tile), lambda i, at: (i, 0, 0, 0)),
        jax.ShapeDtypeStruct((no, n // 2, size, tile), f32),
        [pltpu.VMEM((batch, columns), f32), pltpu.VMEM((2 * batch, columns), bf16)],
        cost(6 * batch * columns * rows, 4 * columns * rows),
        (at, e, s),
        after,
    )


def decode_kernel(part, start, factor, stage, at_ref, y_ref, hi_ref, lo_ref, v_ref, ve_ref, ce_ref, *refs):
    o_ref, whole = refs[-2:]
    batch, vrows, cwidth = o_ref.shape
    tiles, tile = y_ref.shape[0], y_ref.shape[3]

    @pl.when(pl.program_id(0) == 0)
    def _():
        o_ref[...] = refs[0][...] if stage else jnp.zeros_like(o_ref)

    for e in range(tiles):
        if tiles == 1:
            whole[...] = y_ref[e, 0]
        else:
            whole[:, pl.ds(pl.multiple_of((e ^ at_ref[3]) * tile, tile), tile)] = y_ref[e, 0]
    v = v_ref[0]
    chi, clo = hi_ref[0], lo_ref[0]
    for i in range(batch // part):
        y = whole[start + i * part : start + (i + 1) * part, :]
        weighted = (y[:, None, :] * v[None]).reshape(part * vrows, v.shape[1])
        hi, lo = split(weighted)
        got = dot(hi, chi, across) + dot(hi, clo, across) + dot(lo, chi, across)
        o_ref[i * part : (i + 1) * part] += got.reshape(part, vrows, cwidth)

    if factor is not None:

        @pl.when(pl.program_id(0) == pl.num_programs(0) - 1)
        def _():
            shifted = (ce_ref[...] - ve_ref[...]) - center_shift
            result = factor * (o_ref[...] + shifted[None] * refs[stage][...])
            if len(refs) > 3 + stage:
                result = result - refs[stage + 1][...]
            o_ref[...] = result


def decode(y, chi, clo, v, ve, ce, at, amplitudes, first, chunk, chunks, factor, after):
    tiles, pieces, size, tile = y[0].shape
    points = tiles * tile
    batch = size // chunks
    vrows, cwidth = v.shape[1], chi.shape[1]
    own = pl.BlockSpec((batch, vrows, cwidth), lambda p, at: (at[0] * chunks + chunk, 0, at[1]))
    mine = pl.BlockSpec((batch, vrows, cwidth), lambda p, at: (chunk, 0, 0))
    fixed = pl.BlockSpec((batch, vrows, cwidth), lambda p, at: (0, 0, 0))
    blocks = [amplitudes] if first is None else [first, amplitudes]
    total = None
    for stage in range(len(y)):
        last = stage == len(y) - 1

        def piece(p, at, stage=stage):
            return (stage * pieces + p, 0, 0)

        total = call(
            functools.partial(
                decode_kernel, part_of(batch, vrows), chunk * batch, factor if last else None, stage
            ),
            "decode",
            (pieces,),
            [
                pl.BlockSpec((tiles, 1, size, tile), lambda p, at: (0, p, 0, 0)),
                pl.BlockSpec((1, cwidth, points), piece),
                pl.BlockSpec((1, cwidth, points), piece),
                pl.BlockSpec((1, vrows, points), piece),
                pl.BlockSpec((vrows, 1), lambda p, at: (0, 0)),
                pl.BlockSpec((1, cwidth), lambda p, at: (0, at[1])),
            ]
            + [fixed] * stage
            + (([own] if first is None else [mine, own]) if last else []),
            fixed,
            jax.ShapeDtypeStruct((batch, vrows, cwidth), f32),
            [pltpu.VMEM((size, points), f32)],
            cost(6 * batch * vrows * cwidth * points * pieces, 4 * (cwidth + vrows) * points * pieces),
            (at, y[stage], chi, clo, v, ve, ce, *([total] * stage), *(blocks if last else [])),
            after,
        )
        after = ()
    return total


def place_kernel(c_ref, *refs):
    hi_ref, lo_ref, mark_ref = refs[-3:]
    hi, lo = split(c_ref[...])
    hi_ref[0] = hi
    lo_ref[0] = lo
    mark_ref[...] = jnp.zeros_like(mark_ref)


def place(piece, slot, so_far, n):
    cwidth, points = piece.shape
    tile = min(points, 1024)
    carried = [] if so_far is None else list(so_far)
    shape = jax.ShapeDtypeStruct((n, cwidth, points), bf16)
    out = pl.BlockSpec((1, cwidth, tile), lambda j: (slot, 0, j))
    *placed, mark = pl.pallas_call(
        place_kernel,
        grid=(points // tile,),
        in_specs=[pl.BlockSpec((cwidth, tile), lambda j: (0, j))] + [anywhere] * len(carried),
        out_specs=[out, out, pl.BlockSpec((8, 128), lambda j: (0, 0))],
        out_shape=[shape, shape, jax.ShapeDtypeStruct((8, 128), f32)],
        input_output_aliases={1 + i: i for i in range(len(carried))},
        compiler_params=params(),
        cost_estimate=cost(0, 16 * cwidth * points),
        name="place",
    )(piece, *carried)
    return placed, mark


def put_kernel(owners, chunk, chunks, count, at_ref, *refs):
    pieces, (out, mark, held, came, went) = refs[:count], refs[-5:]
    mark[...] = jnp.zeros_like(mark)
    batch, _, cwidth = pieces[0].shape
    arriving = [pltpu.make_async_copy(pieces[i], held.at[i], came.at[i]) for i in range(count)]
    for copy in arriving:
        copy.start()
    leaving = []
    for i, d in enumerate(owners):
        team, half = at_ref[0] ^ group_of(d), at_ref[1] ^ ((d // 2) % 2)
        where = out.at[
            pl.ds((team * chunks + chunk) * batch, batch),
            :,
            pl.ds(pl.multiple_of(half * cwidth, cwidth), cwidth),
        ]
        arriving[i].wait()
        leaving.append(pltpu.make_async_copy(held.at[i], where, went.at[i]))
        leaving[i].start()
    for copy in leaving:
        copy.wait()


def put(pieces, chunk, chunks, at, so_far, shape):
    owners = sorted(pieces)
    count = len(owners)
    carried = [] if so_far is None else [so_far]
    block = pieces[owners[0]].shape
    return pl.pallas_call(
        functools.partial(put_kernel, owners, chunk, chunks, count),
        in_specs=[pl.BlockSpec(memory_space=pltpu.SMEM)] + [anywhere] * (count + len(carried)),
        out_specs=[anywhere, pl.BlockSpec(memory_space=pltpu.VMEM)],
        out_shape=[jax.ShapeDtypeStruct(shape, f32), jax.ShapeDtypeStruct((8, 128), f32)],
        scratch_shapes=[
            pltpu.VMEM((count,) + block, f32),
            pltpu.SemaphoreType.DMA((count,)),
            pltpu.SemaphoreType.DMA((count,)),
        ],
        input_output_aliases={count + 1 + i: i for i in range(len(carried))},
        compiler_params=params(),
        cost_estimate=cost(0, 16 * count * pieces[owners[0]].size),
        name="put",
    )(at, *[pieces[d] for d in owners], *carried)


def flip(x, axis, bit, size):
    return lax.ppermute(x, axis, [(i, i ^ bit) for i in range(size)])


def bits_of(size):
    return [1 << i for i in range(size.bit_length() - 1)]


def reorder(x, dim, by):
    for bit in bits_of(x.shape[dim]):
        shape = x.shape[:dim] + (x.shape[dim] // (2 * bit), 2, bit) + x.shape[dim + 1 :]
        swapped = lax.rev(x.reshape(shape), (dim + 1,)).reshape(x.shape)
        x = jnp.where((by // bit) % 2 == 1, swapped, x)
    return x


def tie(x, after):
    return lax.optimization_barrier((x, after))[0]


def take_bit(x, dim, bit, value):
    shape = x.shape[:dim] + (x.shape[dim] // (2 * bit), 2, bit) + x.shape[dim + 1 :]
    part = lax.index_in_dim(x.reshape(shape), value, dim + 1, keepdims=False)
    return part.reshape(x.shape[:dim] + (x.shape[dim] // 2,) + x.shape[dim + 1 :])


def scatter_sum(x, axis, size):
    for bit in bits_of(size):
        x = take_bit(x, 0, 1, 0) + flip(take_bit(x, 0, 1, 1), axis, bit, size)
    return x[0]


class Comm:
    def __init__(self, n, no):
        self.n, self.no = n, no
        self.me, self.mo = lax.axis_index("pts"), lax.axis_index("orb")
        self.half = (self.me // 2) % 2
        self.member = group_of(self.me)
        self.per = n // no


def slots(order):
    found = [0]
    for bit in order:
        found = found + [d | bit for d in found]
    return found


def spread_bits(n):
    return [2] + [b for b in bits_of(n) if b >= 4] + [1]


def join_kernel(a_ref, b_ref, *refs):
    o_ref = refs[-1]
    o_ref[0] = a_ref[...]
    o_ref[1] = b_ref[...]


def join(a, b, after):
    whole = pl.BlockSpec(memory_space=pltpu.VMEM)
    out = pl.pallas_call(
        join_kernel,
        in_specs=[whole, whole] + [anywhere] * len(after),
        out_specs=whole,
        out_shape=jax.ShapeDtypeStruct((2,) + a.shape, f32),
        compiler_params=params(),
        cost_estimate=cost(0, 16 * a.size),
        name="join",
    )(a, b, *after)
    return out.reshape((2 * a.shape[0],) + a.shape[1:])


def spread_encoded(x, comm, after=()):
    x = x[None]
    for i, bit in enumerate(spread_bits(comm.n)):
        other = flip(x, "pts", bit, comm.n)
        x = join(x, other, after) if after and i == 0 else jnp.concatenate([x, other], axis=0)
    return x


def arrange_kernel(at_ref, x_ref, v_ref, o_ref, copy_ref):
    no, per = o_ref.shape[:2]
    for e in range(no):
        for c in range(per):
            o_ref[e, c] = x_ref[((e ^ at_ref[3]) * per + c) ^ at_ref[2]]
    copy_ref[...] = v_ref[...]


def arrange(x, v, at, no, after):
    n, batch, width = x.shape
    per = n // no
    return call(
        arrange_kernel,
        "arrange",
        (1,),
        [
            pl.BlockSpec((n, batch, width), lambda i, at: (0, 0, 0)),
            pl.BlockSpec(v.shape, lambda i, at: (0, 0)),
        ],
        [
            pl.BlockSpec((no, per, batch, width), lambda i, at: (0, 0, 0, 0)),
            pl.BlockSpec(v.shape, lambda i, at: (0, 0)),
        ],
        [jax.ShapeDtypeStruct((no, per, batch, width), f32), jax.ShapeDtypeStruct(v.shape, f32)],
        [],
        cost(0, 8 * x.size),
        (at, x, v),
        after,
    )


def send_encoded_own(x, v, at, comm, after):
    n, no = comm.n, comm.no
    x = x[None]
    for bit in bits_of(n):
        dim = 1 if bit == 2 else 2
        other = flip(take_bit(x, dim, 1, 1), "pts", bit, n)
        x = jnp.concatenate([take_bit(x, dim, 1, 0), other], axis=0)
    x, v = arrange(x[:, 0, 0], v, at, no, after)
    vpieces = {0: v}
    for bit in [b for b in bits_of(n) if b >= 4] + [2]:
        for d in list(vpieces):
            vpieces[d | bit] = flip(vpieces[d], "pts", bit, n)
    early = tuple(vpieces[b] for b in bits_of(n) if b >= 4)
    return spread_encoded(scatter_sum(x, "orb", no), comm, early), vpieces


def send_encoded_all(send, keep, comm):
    x = keep + flip(send, "pts", 2, comm.n)
    return spread_encoded(scatter_sum(x, "orb", comm.no), comm)


def send_interacted(x, comm, before=None):
    n, no = comm.n, comm.no
    x = x[:, None]
    for bit in [b for b in bits_of(n) if b != 2]:
        other = flip(take_bit(x, 2, 1, 1), "pts", bit, n)
        x = jnp.concatenate([take_bit(x, 2, 1, 0), other], axis=1)
    x = x[:, :, 0]
    if before is not None:
        x = tie(x, before)
    x = scatter_sum(x, "orb", no)[None]
    near, far = {0: x}, {0: flip(x, "pts", 2, n)}
    for bit in reversed(bits_of(no)):
        have = sorted(near)
        more = flip(jnp.concatenate([near[e] for e in have], axis=0), "orb", bit, no)
        side = flip(more, "pts", 2, n)
        for i, e in enumerate(have):
            near[e | bit], far[e | bit] = more[i : i + 1], side[i : i + 1]
    result = []
    for side in (near, far):
        x = jnp.concatenate([side[e] for e in range(no)], axis=0)
        if x.shape[3] % 128:
            x = reorder(x, 0, comm.mo).transpose(1, 2, 0, 3)
            x = x.reshape((1,) + x.shape[:2] + (-1,))
        result.append(x)
    return result


def around(x, order, n):
    own = {bit: flip(x, "pts", bit, n) for bit in order}
    got = {0: x, order[0]: tie(own[order[0]], tuple(own.values()))}
    for bit in order[1:]:
        for d in list(got):
            got[d | bit] = own[bit] if d == 0 else flip(got[d], "pts", bit, n)
    return got


def body(
    amplitudes, valence_points, conduction_points, screened, valence_energy, conduction_energy, n, no
):
    comm = Comm(n, no)
    ve, ce = valence_energy[:, None], conduction_energy[None, :]
    teams = n // 2
    size = amplitudes.shape[0] // teams
    at = jnp.stack([comm.member, comm.half, comm.me, comm.mo]).astype(jnp.int32)

    cwidth = conduction_points.shape[0] // 2
    mine = lax.dynamic_slice_in_dim(conduction_points, comm.half * cwidth, cwidth, 0)
    other = lax.dynamic_slice_in_dim(conduction_points, (1 - comm.half) * cwidth, cwidth, 0)
    high = [b for b in bits_of(n) if b >= 4]


    pieces = {0: mine, 2: flip(other, "pts", 2, n), high[0]: flip(mine, "pts", high[0], n)}
    early = (pieces[2], pieces[high[0]])
    cuts = [0, teams - teams // 4, teams]
    parts, after = [], ()
    for start, end in zip(cuts, cuts[1:]):
        part = encode_own(
            amplitudes, conduction_points, valence_points, at, start, end - start, size, after
        )
        after = (part,) + early
        parts.append(part)
    for bit in high:
        for d in list(pieces):
            if d | bit not in pieces:
                pieces[d | bit] = flip(tie(pieces[d], parts[0]), "pts", bit, n)
    across_x = tuple(pieces[d] for d in pieces if d not in (0, 2, high[0]))
    near = list(pieces)
    placed, marks = None, []
    for d in near:
        placed, mark = place(pieces[d], slot_of(d, n), placed, n)
        marks.append(mark)
        pieces[d | 1] = flip(pieces[d], "pts", 1, n)
    e, vpieces = send_encoded_own(
        jnp.concatenate(parts, axis=1),
        valence_points,
        at,
        comm,
        across_x + tuple(marks[: len(marks) - len(across_x)]),
    )
    got = interact(e, screened, at, after)
    for d in near:
        placed, _ = place(pieces[d | 1], slot_of(d | 1, n), placed, n)

    for d in list(vpieces):
        vpieces[d | 1] = flip(vpieces[d], "pts", 1, n)
    v = jnp.stack([vpieces[d] for d in sorted(vpieces, key=lambda d: slot_of(d, n))])
    chi, clo = placed

    def decoded(y, first, chunk, chunks, factor, after):
        return decode(y, chi, clo, v, ve, ce, at, amplitudes, first, chunk, chunks, factor, after)

    y = send_interacted(got, comm)
    first = decoded(y, None, 0, 1, 0.5, ())
    send = encode_all(first, chi, clo, v, at, 1, n, no, ())
    keep = encode_all(first, chi, clo, v, at, 0, n, no, (send,))
    e = send_encoded_all(send, keep, comm)
    y = send_interacted(interact(e, screened, at, ()), comm)
    out, after, marks = None, (), []
    waiting, decodes = [], []
    both = [jnp.concatenate(y, axis=1)]
    for chunk in range(chunks):
        if chunk >= 2:
            after += tuple(waiting[chunk - 2][b] for b in high + [2])
        if chunk >= 3:
            after += tuple(waiting[chunk - 3].values())
        got = decoded(y if chunk == 0 else both, first, chunk, chunks, 1.0, after)
        after = (got,)
        decodes.append(got)
        waiting.append(around(got, [2] + high if chunk % 2 == 0 else high + [2], n))
    for chunk, blocks in enumerate(waiting):
        for d in list(blocks):
            block = blocks[d]
            if chunk < chunks - 2:
                block = tie(block, decodes[chunk + 2])
            if chunk == chunks - 1:
                block = tie(block, tuple(marks[: chunks - 2]))
            blocks[d | 1] = flip(block, "pts", 1, n)
        if chunk < chunks - 1:
            out, mark = put(blocks, chunk, chunks, at, out, amplitudes.shape)
            marks.append(mark)
        else:
            near = {d: blocks[d] for d in blocks if d % 2 == 0}
            out, _ = put(near, chunk, chunks, at, out, amplitudes.shape)
            far = {d: blocks[d] for d in blocks if d % 2 == 1}
            out, _ = put(far, chunk, chunks, at, out, amplitudes.shape)
    return out


def solution(mesh):
    n, no = mesh.shape["pts"], mesh.shape["orb"]
    return jax.shard_map(
        functools.partial(body, n=n, no=no),
        mesh=mesh,
        in_specs=(
            P(None, "orb", None),
            P("orb", "pts"),
            P(None, "pts"),
            P("pts", "orb"),
            P("orb"),
            P(),
        ),
        out_specs=P(None, "orb", None),
        check_vma=False,
    )
```

```python
import functools

import jax
import jax.numpy as jnp
from jax import lax
from jax.experimental import pallas as pl
from jax.experimental.pallas import tpu as pltpu
from jax.sharding import PartitionSpec as P

center_shift = 2.5
f32, bf16 = jnp.float32, jnp.bfloat16
plain = (((1,), (0,)), ((), ()))
across = (((1,), (1,)), ((), ()))
anywhere = pl.BlockSpec(memory_space=pl.ANY)
vmem_bytes = 56 * 2**20
chunks = 4


def params():
    return pltpu.CompilerParams(vmem_limit_bytes=vmem_bytes)


def cost(flops, nbytes):
    return pl.CostEstimate(flops=flops, bytes_accessed=nbytes, transcendentals=0)


def split(x):
    hi = x.astype(bf16)
    return hi, (x - hi.astype(f32)).astype(bf16)


def dot(a, b, dims=plain):
    return lax.dot_general(a, b, dims, preferred_element_type=f32)


def part_of(batch, rows):
    return max(k for k in range(1, batch + 1) if batch % k == 0 and (k == 1 or k * rows <= 512))


def call(kernel, name, grid, in_specs, out_specs, out_shape, scratch, estimate, args, after):
    count = len(args)

    def run(*refs):
        kernel(*refs[:count], *refs[count + len(after) :])

    return pl.pallas_call(
        run,
        grid_spec=pltpu.PrefetchScalarGridSpec(
            num_scalar_prefetch=1,
            grid=grid,
            in_specs=in_specs + [anywhere] * len(after),
            out_specs=out_specs,
            scratch_shapes=scratch,
        ),
        out_shape=out_shape,
        compiler_params=params(),
        cost_estimate=estimate,
        name=name,
    )(*args, *after)


def encode_own_kernel(part, at_ref, x_ref, c_ref, v_ref, o_ref, xs, cs, whole):
    batch, vrows, cwidth = x_ref.shape
    width = o_ref.shape[3]

    @pl.when(pl.program_id(0) == 0)
    def _():
        hi, lo = split(c_ref[...])
        cs[0:cwidth] = hi
        cs[cwidth : 2 * cwidth] = lo
        cs[2 * cwidth :] = hi

    hi, lo = split(x_ref[...].reshape(batch * vrows, cwidth))
    xs[:, 0:cwidth] = hi
    xs[:, cwidth : 2 * cwidth] = hi
    xs[:, 2 * cwidth :] = lo
    v = v_ref[...]
    for i in range(batch // part):
        prod = dot(xs[i * part * vrows : (i + 1) * part * vrows, :], cs[...])
        prod = prod.reshape(part, vrows, v.shape[1]) * v[None]
        whole[i * part : (i + 1) * part, :] = jnp.sum(prod, axis=1)
    for j in range(2):
        o_ref[j, 0] = whole[:, pl.ds(pl.multiple_of((at_ref[1] ^ j) * width, width), width)]


def encode_own(x, c, v, at, start, count, size, after):
    vrows, cwidth = x.shape[1:]
    points = c.shape[1]
    width = points // 2
    return call(
        functools.partial(encode_own_kernel, part_of(size, vrows)),
        "encode_own",
        (count,),
        [
            pl.BlockSpec((size, vrows, cwidth), lambda i, at: ((start + i) ^ at[0], 0, 0)),
            pl.BlockSpec((cwidth, points), lambda i, at: (0, 0)),
            pl.BlockSpec((vrows, points), lambda i, at: (0, 0)),
        ],
        pl.BlockSpec((2, 1, size, width), lambda i, at: (0, i, 0, 0)),
        jax.ShapeDtypeStruct((2, count, size, width), f32),
        [
            pltpu.VMEM((size * vrows, 3 * cwidth), bf16),
            pltpu.VMEM((3 * cwidth, points), bf16),
            pltpu.VMEM((size, points), f32),
        ],
        cost(size * count * vrows * cwidth * points // 4, size * count * vrows * cwidth // 4),
        (at, x, c, v),
        after,
    )


def encode_all_kernel(part, at_ref, x_ref, hi_ref, lo_ref, v_ref, o_ref, xs):
    del at_ref
    batch, vrows, cwidth = x_ref.shape

    @pl.when((pl.program_id(0) == 0) & (pl.program_id(1) == 0))
    def _():
        hi, lo = split(x_ref[...].reshape(batch * vrows, cwidth))
        xs[:, 0:cwidth] = hi
        xs[:, cwidth : 2 * cwidth] = hi
        xs[:, 2 * cwidth :] = lo

    chi = hi_ref[0]
    w = jnp.concatenate([chi, lo_ref[0], chi], axis=0)
    v = v_ref[0]
    for i in range(batch // part):
        prod = dot(xs[i * part * vrows : (i + 1) * part * vrows, :], w)
        prod = prod.reshape(part, vrows, v.shape[1]) * v[None]
        o_ref[0, 0, i * part : (i + 1) * part, :] = jnp.sum(prod, axis=1)


def slot_of(d, n):
    return group_of(d) + ((d // 2) % 2) * (n // 2)


def group_of(d):
    return (d // 4) * 2 + d % 2


def encode_all(x, chi, clo, v, at, which, n, no, after):
    batch, vrows, cwidth = x.shape
    width = chi.shape[2] // 2
    per = n // no

    def piece(e, c, at):
        return (slot_of(((at[3] ^ e) * per + c) ^ at[2], n), 0, which ^ at[1])

    return call(
        functools.partial(encode_all_kernel, part_of(batch, vrows)),
        "encode_all",
        (no, per),
        [
            pl.BlockSpec((batch, vrows, cwidth), lambda e, c, at: (0, 0, 0)),
            pl.BlockSpec((1, cwidth, width), piece),
            pl.BlockSpec((1, cwidth, width), piece),
            pl.BlockSpec((1, vrows, width), piece),
        ],
        pl.BlockSpec((1, 1, batch, width), lambda e, c, at: (e, c, 0, 0)),
        jax.ShapeDtypeStruct((no, per, batch, width), f32),
        [pltpu.VMEM((batch * vrows, 3 * cwidth), bf16)],
        cost(6 * batch * vrows * cwidth * width * n, 4 * (cwidth + vrows) * width * n),
        (at, x, chi, clo, v),
        after,
    )


def interact_kernel(order, at_ref, e_ref, s_ref, o_ref, whole, es):
    n, per, size, width = e_ref.shape
    batch = whole.shape[0]

    @pl.when(pl.program_id(0) == 0)
    def _():
        for i, d in enumerate(order):
            row = group_of(d) * size
            for c in range(per):
                column = (2 * c + (at_ref[1] ^ ((d // 2) % 2))) * width
                whole[row : row + size, pl.ds(pl.multiple_of(column, width), width)] = e_ref[i, c]
        hi, lo = split(whole[...])
        es[0:batch] = hi
        es[batch:] = lo

    hi, lo = split(s_ref[...])
    both = dot(es[...], hi, across)
    result = both[:batch] + both[batch:] + dot(es[0:batch], lo, across)
    for g in range(batch // size):
        o_ref[0, g] = result[g * size : (g + 1) * size]


def interact(e, s, at, after):
    n, per, size, width = e.shape
    rows, columns = s.shape
    batch = n // 2 * size
    no = n // per
    tile = rows // no
    return call(
        functools.partial(interact_kernel, slots(spread_bits(n))),
        "interact",
        (no,),
        [
            pl.BlockSpec(e.shape, lambda i, at: (0, 0, 0, 0)),
            pl.BlockSpec((tile, columns), lambda i, at: (i ^ at[3], 0)),
        ],
        pl.BlockSpec((1, n // 2, size, tile), lambda i, at: (i, 0, 0, 0)),
        jax.ShapeDtypeStruct((no, n // 2, size, tile), f32),
        [pltpu.VMEM((batch, columns), f32), pltpu.VMEM((2 * batch, columns), bf16)],
        cost(6 * batch * columns * rows // 16, columns * rows // 4),
        (at, e, s),
        after,
    )


def decode_kernel(part, start, factor, stage, at_ref, y_ref, hi_ref, lo_ref, v_ref, ve_ref, ce_ref, *refs):
    o_ref, whole = refs[-2:]
    batch, vrows, cwidth = o_ref.shape
    tiles, tile = y_ref.shape[0], y_ref.shape[3]

    @pl.when(pl.program_id(0) == 0)
    def _():
        o_ref[...] = refs[0][...] if stage else jnp.zeros_like(o_ref)

    for e in range(tiles):
        if tiles == 1:
            whole[...] = y_ref[e, 0]
        else:
            whole[:, pl.ds(pl.multiple_of((e ^ at_ref[3]) * tile, tile), tile)] = y_ref[e, 0]
    v = v_ref[0]
    chi, clo = hi_ref[0], lo_ref[0]
    for i in range(batch // part):
        y = whole[start + i * part : start + (i + 1) * part, :]
        weighted = (y[:, None, :] * v[None]).reshape(part * vrows, v.shape[1])
        hi, lo = split(weighted)
        got = dot(hi, chi, across) + dot(hi, clo, across) + dot(lo, chi, across)
        o_ref[i * part : (i + 1) * part] += got.reshape(part, vrows, cwidth)

    if factor is not None:

        @pl.when(pl.program_id(0) == pl.num_programs(0) - 1)
        def _():
            shifted = (ce_ref[...] - ve_ref[...]) - center_shift
            result = factor * (o_ref[...] + shifted[None] * refs[stage][...])
            if len(refs) > 3 + stage:
                result = result - refs[stage + 1][...]
            o_ref[...] = result


def decode(y, chi, clo, v, ve, ce, at, amplitudes, first, chunk, chunks, factor, after):
    tiles, pieces, size, tile = y[0].shape
    points = tiles * tile
    batch = size // chunks
    vrows, cwidth = v.shape[1], chi.shape[1]
    own = pl.BlockSpec((batch, vrows, cwidth), lambda p, at: (at[0] * chunks + chunk, 0, at[1]))
    mine = pl.BlockSpec((batch, vrows, cwidth), lambda p, at: (chunk, 0, 0))
    fixed = pl.BlockSpec((batch, vrows, cwidth), lambda p, at: (0, 0, 0))
    blocks = [amplitudes] if first is None else [first, amplitudes]
    total = None
    for stage in range(len(y)):
        last = stage == len(y) - 1

        def piece(p, at, stage=stage):
            return (stage * pieces + p, 0, 0)

        total = call(
            functools.partial(
                decode_kernel, part_of(batch, vrows), chunk * batch, factor if last else None, stage
            ),
            "decode",
            (pieces,),
            [
                pl.BlockSpec((tiles, 1, size, tile), lambda p, at: (0, p, 0, 0)),
                pl.BlockSpec((1, cwidth, points), piece),
                pl.BlockSpec((1, cwidth, points), piece),
                pl.BlockSpec((1, vrows, points), piece),
                pl.BlockSpec((vrows, 1), lambda p, at: (0, 0)),
                pl.BlockSpec((1, cwidth), lambda p, at: (0, at[1])),
            ]
            + [fixed] * stage
            + (([own] if first is None else [mine, own]) if last else []),
            fixed,
            jax.ShapeDtypeStruct((batch, vrows, cwidth), f32),
            [pltpu.VMEM((size, points), f32)],
            cost(6 * batch * vrows * cwidth * points * pieces, 4 * (cwidth + vrows) * points * pieces),
            (at, y[stage], chi, clo, v, ve, ce, *([total] * stage), *(blocks if last else [])),
            after,
        )
        after = ()
    return total


def place_kernel(c_ref, *refs):
    hi_ref, lo_ref, mark_ref = refs[-3:]
    hi, lo = split(c_ref[...])
    hi_ref[0] = hi
    lo_ref[0] = lo
    mark_ref[...] = jnp.zeros_like(mark_ref)


def place(piece, slot, so_far, n):
    cwidth, points = piece.shape
    tile = min(points, 1024)
    carried = [] if so_far is None else list(so_far)
    shape = jax.ShapeDtypeStruct((n, cwidth, points), bf16)
    out = pl.BlockSpec((1, cwidth, tile), lambda j: (slot, 0, j))
    *placed, mark = pl.pallas_call(
        place_kernel,
        grid=(points // tile,),
        in_specs=[pl.BlockSpec((cwidth, tile), lambda j: (0, j))] + [anywhere] * len(carried),
        out_specs=[out, out, pl.BlockSpec((8, 128), lambda j: (0, 0))],
        out_shape=[shape, shape, jax.ShapeDtypeStruct((8, 128), f32)],
        input_output_aliases={1 + i: i for i in range(len(carried))},
        compiler_params=params(),
        cost_estimate=cost(0, 16 * cwidth * points),
        name="place",
    )(piece, *carried)
    return placed, mark


def put_kernel(owners, chunk, chunks, count, at_ref, *refs):
    pieces, (out, mark, held, came, went) = refs[:count], refs[-5:]
    mark[...] = jnp.zeros_like(mark)
    batch, _, cwidth = pieces[0].shape
    arriving = [pltpu.make_async_copy(pieces[i], held.at[i], came.at[i]) for i in range(count)]
    for copy in arriving:
        copy.start()
    leaving = []
    for i, d in enumerate(owners):
        team, half = at_ref[0] ^ group_of(d), at_ref[1] ^ ((d // 2) % 2)
        where = out.at[
            pl.ds((team * chunks + chunk) * batch, batch),
            :,
            pl.ds(pl.multiple_of(half * cwidth, cwidth), cwidth),
        ]
        arriving[i].wait()
        leaving.append(pltpu.make_async_copy(held.at[i], where, went.at[i]))
        leaving[i].start()
    for copy in leaving:
        copy.wait()


def put(pieces, chunk, chunks, at, so_far, shape):
    owners = sorted(pieces)
    count = len(owners)
    carried = [] if so_far is None else [so_far]
    block = pieces[owners[0]].shape
    return pl.pallas_call(
        functools.partial(put_kernel, owners, chunk, chunks, count),
        in_specs=[pl.BlockSpec(memory_space=pltpu.SMEM)] + [anywhere] * (count + len(carried)),
        out_specs=[anywhere, pl.BlockSpec(memory_space=pltpu.VMEM)],
        out_shape=[jax.ShapeDtypeStruct(shape, f32), jax.ShapeDtypeStruct((8, 128), f32)],
        scratch_shapes=[
            pltpu.VMEM((count,) + block, f32),
            pltpu.SemaphoreType.DMA((count,)),
            pltpu.SemaphoreType.DMA((count,)),
        ],
        input_output_aliases={count + 1 + i: i for i in range(len(carried))},
        compiler_params=params(),
        cost_estimate=cost(0, 16 * count * pieces[owners[0]].size),
        name="put",
    )(at, *[pieces[d] for d in owners], *carried)


def flip(x, axis, bit, size):
    return lax.ppermute(x, axis, [(i, i ^ bit) for i in range(size)])


def bits_of(size):
    return [1 << i for i in range(size.bit_length() - 1)]


def reorder(x, dim, by):
    for bit in bits_of(x.shape[dim]):
        shape = x.shape[:dim] + (x.shape[dim] // (2 * bit), 2, bit) + x.shape[dim + 1 :]
        swapped = lax.rev(x.reshape(shape), (dim + 1,)).reshape(x.shape)
        x = jnp.where((by // bit) % 2 == 1, swapped, x)
    return x


def tie(x, after):
    return lax.optimization_barrier((x, after))[0]


def take_bit(x, dim, bit, value):
    shape = x.shape[:dim] + (x.shape[dim] // (2 * bit), 2, bit) + x.shape[dim + 1 :]
    part = lax.index_in_dim(x.reshape(shape), value, dim + 1, keepdims=False)
    return part.reshape(x.shape[:dim] + (x.shape[dim] // 2,) + x.shape[dim + 1 :])


def scatter_sum(x, axis, size):
    for bit in bits_of(size):
        x = take_bit(x, 0, 1, 0) + flip(take_bit(x, 0, 1, 1), axis, bit, size)
    return x[0]


class Comm:
    def __init__(self, n, no):
        self.n, self.no = n, no
        self.me, self.mo = lax.axis_index("pts"), lax.axis_index("orb")
        self.half = (self.me // 2) % 2
        self.member = group_of(self.me)
        self.per = n // no


def slots(order):
    found = [0]
    for bit in order:
        found = found + [d | bit for d in found]
    return found


def spread_bits(n):
    return [2] + [b for b in bits_of(n) if b >= 4] + [1]


def join_kernel(a_ref, b_ref, *refs):
    o_ref = refs[-1]
    o_ref[0] = a_ref[...]
    o_ref[1] = b_ref[...]


def join(a, b, after):
    whole = pl.BlockSpec(memory_space=pltpu.VMEM)
    out = pl.pallas_call(
        join_kernel,
        in_specs=[whole, whole] + [anywhere] * len(after),
        out_specs=whole,
        out_shape=jax.ShapeDtypeStruct((2,) + a.shape, f32),
        compiler_params=params(),
        cost_estimate=cost(0, 16 * a.size),
        name="join",
    )(a, b, *after)
    return out.reshape((2 * a.shape[0],) + a.shape[1:])


def spread_encoded(x, comm, after=()):
    x = x[None]
    for i, bit in enumerate(spread_bits(comm.n)):
        other = flip(x, "pts", bit, comm.n)
        x = join(x, other, after) if after and i == 0 else jnp.concatenate([x, other], axis=0)
    return x


def arrange_kernel(at_ref, x_ref, v_ref, o_ref, copy_ref):
    no, per = o_ref.shape[:2]
    for e in range(no):
        for c in range(per):
            o_ref[e, c] = x_ref[((e ^ at_ref[3]) * per + c) ^ at_ref[2]]
    copy_ref[...] = v_ref[...]


def arrange(x, v, at, no, after):
    n, batch, width = x.shape
    per = n // no
    return call(
        arrange_kernel,
        "arrange",
        (1,),
        [
            pl.BlockSpec((n, batch, width), lambda i, at: (0, 0, 0)),
            pl.BlockSpec(v.shape, lambda i, at: (0, 0)),
        ],
        [
            pl.BlockSpec((no, per, batch, width), lambda i, at: (0, 0, 0, 0)),
            pl.BlockSpec(v.shape, lambda i, at: (0, 0)),
        ],
        [jax.ShapeDtypeStruct((no, per, batch, width), f32), jax.ShapeDtypeStruct(v.shape, f32)],
        [],
        cost(0, 8 * x.size),
        (at, x, v),
        after,
    )


def send_encoded_own(x, v, at, comm, after):
    n, no = comm.n, comm.no
    x = x[None]
    for bit in bits_of(n):
        dim = 1 if bit == 2 else 2
        other = flip(take_bit(x, dim, 1, 1), "pts", bit, n)
        x = jnp.concatenate([take_bit(x, dim, 1, 0), other], axis=0)
    x, v = arrange(x[:, 0, 0], v, at, no, after)
    vpieces = {0: v}
    for bit in [b for b in bits_of(n) if b >= 4] + [2]:
        for d in list(vpieces):
            vpieces[d | bit] = flip(vpieces[d], "pts", bit, n)
    early = tuple(vpieces[b] for b in bits_of(n) if b >= 4)
    return spread_encoded(scatter_sum(x, "orb", no), comm, early), vpieces


def send_encoded_all(send, keep, comm):
    x = keep + flip(send, "pts", 2, comm.n)
    return spread_encoded(scatter_sum(x, "orb", comm.no), comm)


def send_interacted(x, comm, before=None):
    n, no = comm.n, comm.no
    x = x[:, None]
    for bit in [b for b in bits_of(n) if b != 2]:
        other = flip(take_bit(x, 2, 1, 1), "pts", bit, n)
        x = jnp.concatenate([take_bit(x, 2, 1, 0), other], axis=1)
    x = x[:, :, 0]
    if before is not None:
        x = tie(x, before)
    x = scatter_sum(x, "orb", no)[None]
    near, far = {0: x}, {0: flip(x, "pts", 2, n)}
    for bit in reversed(bits_of(no)):
        have = sorted(near)
        more = flip(jnp.concatenate([near[e] for e in have], axis=0), "orb", bit, no)
        side = flip(more, "pts", 2, n)
        for i, e in enumerate(have):
            near[e | bit], far[e | bit] = more[i : i + 1], side[i : i + 1]
    result = []
    for side in (near, far):
        x = jnp.concatenate([side[e] for e in range(no)], axis=0)
        if x.shape[3] % 128:
            x = reorder(x, 0, comm.mo).transpose(1, 2, 0, 3)
            x = x.reshape((1,) + x.shape[:2] + (-1,))
        result.append(x)
    return result


def around(x, order, n):
    own = {bit: flip(x, "pts", bit, n) for bit in order}
    got = {0: x, order[0]: tie(own[order[0]], tuple(own.values()))}
    for bit in order[1:]:
        for d in list(got):
            got[d | bit] = own[bit] if d == 0 else flip(got[d], "pts", bit, n)
    return got


def body(
    amplitudes, valence_points, conduction_points, screened, valence_energy, conduction_energy, n, no
):
    comm = Comm(n, no)
    ve, ce = valence_energy[:, None], conduction_energy[None, :]
    teams = n // 2
    size = amplitudes.shape[0] // teams
    at = jnp.stack([comm.member, comm.half, comm.me, comm.mo]).astype(jnp.int32)

    cwidth = conduction_points.shape[0] // 2
    mine = lax.dynamic_slice_in_dim(conduction_points, comm.half * cwidth, cwidth, 0)
    other = lax.dynamic_slice_in_dim(conduction_points, (1 - comm.half) * cwidth, cwidth, 0)
    high = [b for b in bits_of(n) if b >= 4]


    pieces = {0: mine, 2: flip(other, "pts", 2, n), high[0]: flip(mine, "pts", high[0], n)}
    early = (pieces[2], pieces[high[0]])
    cuts = [0, teams - teams // 4, teams]
    parts, after = [], ()
    for start, end in zip(cuts, cuts[1:]):
        part = encode_own(
            amplitudes, conduction_points, valence_points, at, start, end - start, size, after
        )
        after = (part,) + early
        parts.append(part)
    for bit in high:
        for d in list(pieces):
            if d | bit not in pieces:
                pieces[d | bit] = flip(tie(pieces[d], parts[0]), "pts", bit, n)
    across_x = tuple(pieces[d] for d in pieces if d not in (0, 2, high[0]))
    near = list(pieces)
    placed, marks = None, []
    for d in near:
        placed, mark = place(pieces[d], slot_of(d, n), placed, n)
        marks.append(mark)
        pieces[d | 1] = flip(pieces[d], "pts", 1, n)
    e, vpieces = send_encoded_own(
        jnp.concatenate(parts, axis=1),
        valence_points,
        at,
        comm,
        across_x + tuple(marks[: len(marks) - len(across_x)]),
    )
    got = interact(e, screened, at, after)
    for d in near:
        placed, _ = place(pieces[d | 1], slot_of(d | 1, n), placed, n)

    for d in list(vpieces):
        vpieces[d | 1] = flip(vpieces[d], "pts", 1, n)
    v = jnp.stack([vpieces[d] for d in sorted(vpieces, key=lambda d: slot_of(d, n))])
    chi, clo = placed

    def decoded(y, first, chunk, chunks, factor, after):
        return decode(y, chi, clo, v, ve, ce, at, amplitudes, first, chunk, chunks, factor, after)

    y = send_interacted(got, comm)
    first = decoded(y, None, 0, 1, 0.5, ())
    send = encode_all(first, chi, clo, v, at, 1, n, no, ())
    keep = encode_all(first, chi, clo, v, at, 0, n, no, (send,))
    e = send_encoded_all(send, keep, comm)
    y = send_interacted(interact(e, screened, at, ()), comm)
    out, after, marks = None, (), []
    waiting, decodes = [], []
    both = [jnp.concatenate(y, axis=1)]
    for chunk in range(chunks):
        if chunk >= 2:
            after += tuple(waiting[chunk - 2][b] for b in high + [2])
        if chunk >= 3:
            after += tuple(waiting[chunk - 3].values())
        got = decoded(y if chunk == 0 else both, first, chunk, chunks, 1.0, after)
        after = (got,)
        decodes.append(got)
        waiting.append(around(got, [2] + high if chunk % 2 == 0 else high + [2], n))
    for chunk, blocks in enumerate(waiting):
        for d in list(blocks):
            block = blocks[d]
            if chunk < chunks - 2:
                block = tie(block, decodes[chunk + 2])
            if chunk == chunks - 1:
                block = tie(block, tuple(marks[: chunks - 2]))
            blocks[d | 1] = flip(block, "pts", 1, n)
        if chunk < chunks - 1:
            out, mark = put(blocks, chunk, chunks, at, out, amplitudes.shape)
            marks.append(mark)
        else:
            near = {d: blocks[d] for d in blocks if d % 2 == 0}
            out, _ = put(near, chunk, chunks, at, out, amplitudes.shape)
            far = {d: blocks[d] for d in blocks if d % 2 == 1}
            out, _ = put(far, chunk, chunks, at, out, amplitudes.shape)
    return out


def solution(mesh):
    n, no = mesh.shape["pts"], mesh.shape["orb"]
    return jax.shard_map(
        functools.partial(body, n=n, no=no),
        mesh=mesh,
        in_specs=(
            P(None, "orb", None),
            P("orb", "pts"),
            P(None, "pts"),
            P("pts", "orb"),
            P("orb"),
            P(),
        ),
        out_specs=P(None, "orb", None),
        check_vma=False,
    )
```
